128 devices in a mesh: dp: 4 (over x), seq: 32 (over y, z, core).
Axes of the slice: x: 4, y: 4, z: 4, core: 2. Of those that a mesh axis runs over, the one named last changes fastest.
Arguments:
- residual_in: bfloat16 [4, 4096, 4096], P('dp', 'seq'), may hold values from -6 to 6
- se_streams: bfloat16 [4, 4096, 12288], P('dp', 'seq'), may hold values from -6 to 6
- cotangent: bfloat16 [4, 4096, 4096], P('dp', 'seq'), may hold values from -6 to 6
- feat_short: float32 [3, 12288], replicated, may hold values from -3.5 to 3.5
- feat_medium: float32 [3, 12288], replicated, may hold values from -3.5 to 3.5
- short_filter: float32 [7, 4096], replicated, may hold values from -2 to 2
- medium_filter_weight: bfloat16 [128, 256], replicated, may hold values from -0.5 to 0.5
Outputs:
- grad_residual: bfloat16 [4, 4096, 4096], P('dp', 'seq')
- grad_streams: bfloat16 [4, 4096, 12288], P('dp', 'seq')
- grad_feat_short: float32 [3, 12288], P(None, 'seq')
- grad_feat_medium: float32 [3, 12288], P(None, 'seq')
- grad_short_filter: float32 [7, 4096], P(None, 'seq')
- grad_medium_filter: float32 [128, 256], P(None, 'seq')
The draws below stay inside these ranges and needn't reach their ends.
All inputs are finite; a program needn't handle non-finite values.
Results may differ from the reference program's by a relative error of at most 0.011.
Values may be sent and summed in bfloat16 or wider, within the bound.
No kernel may reach another device: no remote copies, remote signals or barrier semaphores. Data moves between devices by JAX's collectives and lax.ppermute only.
A program may use at most 320 MiB of HBM per device.

```python
import math
import jax
import jax.numpy as jnp
import numpy as np
from jax import lax

D = 4096
KF = 7
KFE = 3
MEDIUM_TAPS = 128
MEDIUM_GROUPS = 256
SLAB = 4096
NSLAB = 4


def spiked(entries, stream_key, source, target, shards_of, factor):
    owner, partner = [(jnp.arange(entries.shape[dim]) // (entries.shape[dim] // shards_of)).reshape([-1 if axis == dim else 1 for axis in range(entries.ndim)]) for dim in (source, target)]
    chosen = jax.random.permutation(stream_key, shards_of)[partner]
    strong = (owner == chosen) | (owner == (partner + shards_of // 2) % shards_of)
    return jnp.where(strong, factor * entries, entries)


def block_scale(stream_key, dims, pieces, low, high):
    def one(position, shards_of):
        steps = jax.random.uniform(jax.random.fold_in(jax.random.fold_in(stream_key, 6), position), (shards_of,), jnp.float32, low / len(pieces), high / len(pieces))
        return jnp.repeat(jnp.exp(steps), dims[position] // shards_of).reshape((-1,) + (1,) * (len(dims) - position - 1))

    loudness = one(*pieces[0])
    for cut in pieces[1:]:
        loudness = loudness * one(*cut)
    return loudness


def normal_values(key, shape, width, bound, split=(), kind=jnp.bfloat16):
    drawn = width * jax.random.normal(key, shape, jnp.float32)
    if split:
        drawn = drawn * block_scale(key, shape, split, -0.22, 0.18)
    return jnp.clip(drawn, -bound, bound).astype(kind)


def noise_with(stream_key, extent, width, most, cuts, heavy, kind=jnp.bfloat16):
    entries = width * jax.random.normal(stream_key, extent, jnp.float32)
    if cuts:
        entries = entries * block_scale(stream_key, extent, cuts, -0.22, 0.18)
    return jnp.clip(spiked(entries, jax.random.fold_in(stream_key, 3), *heavy), -most, most).astype(kind)


def setup_inputs(seed: int = 0) -> dict:
    key_of = jax.random.split(jax.random.key(seed), 8)
    return {
        "residual_in": normal_values(key_of[0], (NSLAB, SLAB, D), 1.0, 6.0, ((0, 4), (1, 32))),
        "se_streams": normal_values(key_of[1], (NSLAB, SLAB, 3 * D), 1.0, 6.0, ((0, 4), (1, 32))),
        "cotangent": noise_with(key_of[2], (NSLAB, SLAB, D), 1.0, 6.0, ((0, 4), (1, 32)), (1, 2, 32, 2.75)),
        "feat_short": normal_values(key_of[3], (KFE, 3 * D), KFE ** -0.5, 3.5, (), jnp.float32),
        "feat_medium": normal_values(key_of[4], (KFE, 3 * D), KFE ** -0.5, 3.5, (), jnp.float32),
        "short_filter": normal_values(key_of[5], (KF, D), KF ** -0.5, 2.0, (), jnp.float32),
        "medium_filter_weight": normal_values(key_of[6], (MEDIUM_TAPS, MEDIUM_GROUPS), MEDIUM_TAPS ** -0.5, 0.5),
    }


def causal_sum(filters, extended_rows, tok_rows):
    length = filters.shape[0]
    summed = filters[0] * extended_rows[length - 1:length - 1 + tok_rows]
    for offset in range(1, length):
        summed = summed + filters[offset] * extended_rows[length - 1 - offset:length - 1 - offset + tok_rows]
    return summed

def ahead_sum(filters, extended_rows, tok_rows):
    summed = filters[0] * extended_rows[0:tok_rows]
    for offset in range(1, filters.shape[0]):
        summed = summed + filters[offset] * extended_rows[offset:offset + tok_rows]
    return summed

def tap_gradient(gradient_rows, history, length):
    tok_rows = gradient_rows.shape[0]
    return jnp.stack([lax.optimization_barrier(jnp.sum(gradient_rows * history[length - 1 - offset:length - 1 - offset + tok_rows], axis=0)) for offset in range(length)])

def band_matrix(filters, tok_rows, lagging):
    length, groups = filters.shape
    in_span = tok_rows + length - 1
    out_pos = np.arange(tok_rows)[:, None]
    input_position = np.arange(in_span)[None, :]
    lag_index = out_pos + length - 1 - input_position if lagging else input_position - out_pos
    inside = (lag_index >= 0) & (lag_index < length)
    clipped = np.clip(lag_index, 0, length - 1).reshape(-1)
    picked = jnp.take(filters.T, jnp.asarray(clipped, dtype=jnp.int32), axis=1).reshape(groups, tok_rows, in_span)
    return jnp.where(jnp.asarray(inside)[None], picked, jnp.zeros((), filters.dtype))

def medium_apply(filters, values, lagging):
    length, groups = filters.shape
    slab_rows, channels = values.shape
    in_span = 2 * length - 1
    toeplitz = band_matrix(filters, length, lagging).astype(jnp.float32)
    zeros_part = jnp.zeros((length - 1, channels), jnp.float32)
    wide = values.astype(jnp.float32)
    padded = jnp.concatenate([zeros_part, wide], 0) if lagging else jnp.concatenate([wide, zeros_part], 0)

    def one_block(block_index):
        extended_rows = lax.dynamic_slice_in_dim(padded, block_index * length, in_span, 0)
        result_rows = jnp.einsum('gte,egc->tgc', toeplitz, extended_rows.reshape(in_span, groups, channels // groups), precision=lax.Precision.HIGHEST)
        return result_rows.reshape(length, channels)
    return lax.map(one_block, jnp.arange(slab_rows // length, dtype=jnp.int32)).reshape(slab_rows, channels)

def medium_gradient(gradient_rows, values, length, groups):
    slab_rows, channels = values.shape
    in_span = 2 * length - 1
    padded = jnp.concatenate([jnp.zeros((length - 1, channels), jnp.float32), values.astype(jnp.float32)], 0)
    grad_wide = gradient_rows.astype(jnp.float32)
    out_pos = np.arange(length)[:, None]
    offsets = np.arange(length)[None, :]
    flat_index = jnp.asarray((out_pos * in_span + out_pos + length - 1 - offsets).reshape(-1), dtype=jnp.int32)

    def one_block(block_index):
        extended_rows = lax.dynamic_slice_in_dim(padded, block_index * length, in_span, 0)
        piece = lax.dynamic_slice_in_dim(grad_wide, block_index * length, length, 0)
        cross_terms = jnp.einsum('tgc,egc->gte', piece.reshape(length, groups, channels // groups), extended_rows.reshape(in_span, groups, channels // groups), precision=lax.Precision.HIGHEST)
        picked = jnp.take(cross_terms.reshape(groups, length * in_span), flat_index, axis=1).reshape(groups, length, length)
        return lax.optimization_barrier(jnp.sum(picked, axis=1)).T
    return lax.optimization_barrier(jnp.sum(lax.map(one_block, jnp.arange(slab_rows // length, dtype=jnp.int32)), axis=0))

def slab_terms(base_rows, streams, cotangent, feat_short, feat_medium, short_filter, medium_filter_weight):
    slab_rows, channels = base_rows.shape
    feat_len = feat_short.shape[0]
    short_len = short_filter.shape[0]
    groups = medium_filter_weight.shape[1]
    streams_ext = jnp.concatenate([jnp.zeros((feat_len - 1 + short_len - 1, 3 * channels), jnp.float32), streams.astype(jnp.float32)], 0)
    featured = causal_sum(feat_short, streams_ext, slab_rows + short_len - 1)
    query_se = featured[short_len - 1:, :channels]
    key_se = featured[:, channels:2 * channels]
    value_se = featured[:, 2 * channels:]
    product_se = key_se * value_se
    filtered_se = causal_sum(short_filter, product_se, slab_rows)
    middle = (base_rows.astype(jnp.float32) + query_se * filtered_se).astype(jnp.bfloat16)
    mid_hist = jnp.concatenate([jnp.zeros((feat_len - 1, channels), jnp.float32), middle.astype(jnp.float32)], 0)
    mid_triple = jnp.concatenate([mid_hist, mid_hist, mid_hist], 1)
    mixed = causal_sum(feat_medium, mid_triple, slab_rows)
    query_mr = mixed[:, :channels]
    key_mr = mixed[:, channels:2 * channels]
    value_mr = mixed[:, 2 * channels:]
    product_mr = (key_mr * value_mr).astype(jnp.bfloat16)
    filtered_mr = medium_apply(medium_filter_weight, product_mr, True)
    upstream = cotangent.astype(jnp.float32)
    grad_query_mr = upstream * filtered_mr
    grad_filtered_mr = (upstream * query_mr).astype(jnp.bfloat16)
    grad_product_mr = medium_apply(medium_filter_weight, grad_filtered_mr, False)
    grad_medium = medium_gradient(grad_filtered_mr, product_mr, medium_filter_weight.shape[0], groups)
    grad_mixed = jnp.concatenate([grad_query_mr, grad_product_mr * value_mr, grad_product_mr * key_mr], 1)
    zeros_tail = jnp.zeros((feat_len - 1, 3 * channels), jnp.float32)
    back_mixed = ahead_sum(feat_medium, jnp.concatenate([grad_mixed, zeros_tail], 0), slab_rows)
    grad_middle = upstream + back_mixed[:, :channels] + back_mixed[:, channels:2 * channels] + back_mixed[:, 2 * channels:]
    grad_feat_mr = tap_gradient(grad_mixed, mid_triple, feat_len)
    grad_query_se = grad_middle * filtered_se
    grad_filtered_se = grad_middle * query_se
    short_product_gradient = ahead_sum(short_filter, jnp.concatenate([grad_filtered_se, jnp.zeros((short_len - 1, channels), jnp.float32)], 0), slab_rows)
    grad_short = tap_gradient(grad_filtered_se, product_se, short_len)
    grad_featured = jnp.concatenate([grad_query_se, short_product_gradient * value_se[short_len - 1:], short_product_gradient * key_se[short_len - 1:]], 1)
    grad_stream_rows = ahead_sum(feat_short, jnp.concatenate([grad_featured, zeros_tail], 0), slab_rows)
    grad_feat_se = tap_gradient(grad_featured, streams_ext[short_len - 1:], feat_len)
    return (grad_middle.astype(jnp.bfloat16), grad_stream_rows.astype(jnp.bfloat16), grad_feat_se, grad_feat_mr, grad_short, grad_medium)

def reference(residual_in, se_streams, cotangent, feat_short, feat_medium, short_filter, medium_filter_weight):

    def per_slab(items):
        return slab_terms(items[0], items[1], items[2], feat_short, feat_medium, short_filter, medium_filter_weight)
    results = lax.map(per_slab, (residual_in, se_streams, cotangent))
    norm_factor = 1.0 / math.sqrt(residual_in.shape[0] * residual_in.shape[1])
    return (results[0], results[1], lax.optimization_barrier(jnp.sum(results[2], axis=0)) * norm_factor, lax.optimization_barrier(jnp.sum(results[3], axis=0)) * norm_factor, lax.optimization_barrier(jnp.sum(results[4], axis=0)) * norm_factor, lax.optimization_barrier(jnp.sum(results[5], axis=0)) * norm_factor)
```

```python
import functools
import math

import jax
import jax.numpy as jnp
from jax import lax
from jax.experimental import pallas as pl
from jax.experimental.pallas import tpu as pltpu
from jax.sharding import PartitionSpec as P

F32 = jnp.float32
BF16 = jnp.bfloat16
LANES = 128
GROUP = 16
BLOCKS = LANES // GROUP
EDGE = 10
FRAME = 24
TILES = 4


def shift_rows(array, axis, by):
    peers = lax.axis_size(axis)
    return lax.ppermute(array, axis, [(i, i + by) for i in range(peers) if 0 <= i + by < peers])


def lane_blocks(shape):
    return lax.broadcasted_iota(jnp.int32, shape, 1) // GROUP


def swap_blocks(parts):
    parts = list(parts)
    block = lane_blocks(parts[0].shape)
    step = BLOCKS // 2
    while step:
        low = (block & step) == 0
        shift = GROUP * step
        for i in range(BLOCKS):
            if i & step == 0:
                first, second = parts[i], parts[i + step]
                parts[i] = jnp.where(low, first, pltpu.roll(second, shift, 1))
                parts[i + step] = jnp.where(low, pltpu.roll(first, LANES - shift, 1), second)
        step //= 2
    return parts


def taps_of(ref, lanes):
    return [ref[i : i + 1, lanes] for i in range(ref.shape[0])]


def back_taps(taps, ref, start, rows):
    total = taps[0] * ref[start : start + rows, :]
    for i in range(1, len(taps)):
        total = total + taps[i] * ref[start - i : start - i + rows, :]
    return total


def ahead_taps(taps, ref, start, rows):
    total = taps[0] * ref[start : start + rows, :]
    for i in range(1, len(taps)):
        total = total + taps[i] * ref[start + i : start + i + rows, :]
    return total


def first_kernel(rows, *refs):
    (q, k, v, res, g, pq, pk, pv, pr, nq, nk, nv, nr, ng) = refs[:14]
    (fsq, fsk, fsv, short, fmq, fmk, fmv) = refs[14:21]
    (w_own, w_edge, d_own, mid_out, q1_out, s1_out, k1_out, v1_out) = refs[21:29]
    (sq, sk, sv, sr, sg, sw, sm) = refs[29:]
    total = rows + GROUP

    @pl.when(pl.program_id(0) == 0)
    def _():
        for ref in (sq, sk, sv, sr, sg):
            ref[...] = jnp.zeros(ref.shape, F32)

    def one_tile(i, carry):
        lanes = pl.ds(pl.multiple_of(i * LANES, LANES), LANES)
        for scratch, own, before, after in (
            (sq, q, pq, nq),
            (sk, k, pk, nk),
            (sv, v, pv, nv),
            (sr, res, pr, nr),
            (sg, g, None, ng),
        ):
            if before is not None:
                scratch[FRAME - EDGE : FRAME, :] = before[:, lanes].astype(F32)
            for r in range(0, rows, GROUP):
                scratch[FRAME + r : FRAME + r + GROUP, :] = own[r : r + GROUP, lanes].astype(F32)
            scratch[FRAME + rows : FRAME + rows + EDGE, :] = after[:, lanes].astype(F32)
        tq, tk, tv = taps_of(fsq, lanes), taps_of(fsk, lanes), taps_of(fsv, lanes)
        for t in range(-GROUP, total, GROUP):
            at = FRAME + t
            k1 = back_taps(tk, sk, at, GROUP)
            v1 = back_taps(tv, sv, at, GROUP)
            sw[at : at + GROUP, :] = k1 * v1
            k1_out[i, t + GROUP : t + 2 * GROUP, :] = k1.astype(BF16)
            v1_out[i, t + GROUP : t + 2 * GROUP, :] = v1.astype(BF16)
        ts = taps_of(short, lanes)
        for t in range(-GROUP, total, GROUP):
            at = FRAME + t
            q1 = back_taps(tq, sq, at, GROUP)
            s1 = back_taps(ts, sw, at, GROUP)
            mid = (sr[at : at + GROUP, :] + q1 * s1).astype(BF16)
            sm[at : at + GROUP, :] = mid.astype(F32)
            mid_out[i, t + GROUP : t + 2 * GROUP, :] = mid
            if t >= 0:
                q1_out[i, t : t + GROUP, :] = q1.astype(BF16)
                s1_out[i, t : t + GROUP, :] = s1.astype(BF16)
        mq, mk, mv = taps_of(fmq, lanes), taps_of(fmk, lanes), taps_of(fmv, lanes)
        products, slopes = [], []
        for t in range(0, total, GROUP):
            at = FRAME + t
            m = [sm[at - j : at - j + GROUP, :] for j in range(3)]
            q2, k2, v2 = [
                taps[0] * m[0] + taps[1] * m[1] + taps[2] * m[2] for taps in (mq, mk, mv)
            ]
            products.append((k2 * v2).astype(BF16))
            slopes.append((sg[at : at + GROUP, :] * q2).astype(BF16))
        for j, part in enumerate(swap_blocks(products[:BLOCKS])):
            w_own[i, j * GROUP : (j + 1) * GROUP, :] = part
        w_edge[i] = products[BLOCKS]
        for j, part in enumerate(swap_blocks(slopes[:BLOCKS])):
            d_own[i, j * GROUP : (j + 1) * GROUP, :] = part
        d_own[i, rows : rows + GROUP, :] = slopes[BLOCKS]
        return carry

    lax.fori_loop(0, TILES, one_tile, 0)


def windows(low, high, last, block):
    rows = []
    for k in range(BLOCKS + 1):
        if k == 0:
            first, second = low, high
        elif k == BLOCKS:
            first, second = high, last
        else:
            shift = LANES - GROUP * k
            second = pltpu.roll(high, shift, 1)
            first = jnp.where(block < BLOCKS - k, pltpu.roll(low, shift, 1), second)
        rows.append(jnp.concatenate([first, second], 1))
    return jnp.concatenate(rows, 0)


def second_kernel(rows, channels, *refs):
    (q, k, v, g, pq, pk, pv, ng) = refs[:8]
    (w_own, w_edge, w_prev, d_own, d_next, taps_fwd, taps_rev) = refs[8:15]
    (mid_in, q1_in, s1_in, k1_in, v1_in) = refs[15:20]
    (fsq, fsk, fsv, short, fmq, fmk, fmv) = refs[20:27]
    (grad_res, grad_streams, sums) = refs[27:30]
    (sq, sk, sv, sg, sm, sw, dq, dk, dv, d1, eq, ek, ev, out_buf, sems) = refs[30:]
    step = pl.program_id(0)
    steps = pl.num_programs(0)
    slot = lax.rem(step, 2)
    width = TILES * LANES
    base = GROUP

    def copies(at_step, at_slot):
        return [
            pltpu.make_async_copy(
                out_buf.at[at_slot, x],
                grad_streams.at[
                    :, pl.ds(pl.multiple_of(x * channels + at_step * width, width), width)
                ],
                sems.at[at_slot, x],
            )
            for x in range(3)
        ]

    @pl.when(step == 0)
    def _():
        for ref in (sg, dq, dk, dv, d1, eq, ek, ev):
            ref[...] = jnp.zeros(ref.shape, F32)

    @pl.when(step >= 2)
    def _():
        for copy in copies(step - 2, slot):
            copy.wait()

    iota_row = lax.broadcasted_iota(jnp.int32, (GROUP, LANES), 0)
    iota_lane = lax.broadcasted_iota(jnp.int32, (GROUP, LANES), 1)

    def one_tile(i, carry):
        lanes = pl.ds(pl.multiple_of(i * LANES, LANES), LANES)
        tile = step * TILES + i
        block = lane_blocks((GROUP, LANES))
        s2_parts, w2_parts = [], []
        s2_last = jnp.zeros((GROUP, LANES), BF16)
        w2_last = jnp.zeros((GROUP, LANES), BF16)
        edge_w = w_edge[i]
        edge_d = d_next[i, rows : rows + GROUP, :]
        for j in range(BLOCKS):
            part = slice(j * GROUP, (j + 1) * GROUP)
            fwd = jnp.broadcast_to(taps_fwd[pl.ds(i * BLOCKS + j, 1), :], (GROUP, LANES))
            rev = jnp.broadcast_to(taps_rev[pl.ds(i * BLOCKS + j, 1), :], (GROUP, LANES))
            fwd = pltpu.roll(fwd, 0, 1, stride=1, stride_axis=0)
            rev = pltpu.roll(rev, 1, 1, stride=1, stride_axis=0)
            ahead = jnp.concatenate(
                [
                    jnp.where(iota_lane >= iota_row, fwd, 0.0),
                    jnp.where(iota_lane < iota_row, fwd, 0.0)[:, :GROUP],
                ],
                1,
            ).astype(BF16)
            lag = jnp.concatenate(
                [
                    jnp.where(iota_lane > iota_row, rev, 0.0),
                    jnp.where(iota_lane <= iota_row, rev, 0.0)[:, :GROUP],
                ],
                1,
            ).astype(BF16)
            turn = (LANES - GROUP * j) % LANES
            own_d = d_own[i, part, :]
            win = windows(
                w_prev[i, part, :],
                w_own[i, part, :],
                pltpu.roll(edge_w, turn, 1) if turn else edge_w,
                block,
            )
            s2 = jnp.dot(lag, win, preferred_element_type=F32).astype(BF16)
            cross = lax.dot_general(
                own_d, win[:, :LANES], (((1,), (1,)), ((), ())), preferred_element_type=F32
            )
            win = windows(
                own_d,
                d_next[i, part, :],
                pltpu.roll(edge_d, turn, 1) if turn else edge_d,
                block,
            )
            w2 = jnp.dot(ahead, win, preferred_element_type=F32).astype(BF16)
            s2_parts.append(s2[:, :LANES])
            w2_parts.append(w2[:, :LANES])
            here = block == j
            s2_end, w2_end = s2[:, LANES:], w2[:, LANES:]
            if j:
                s2_end, w2_end = (
                    pltpu.roll(s2_end, GROUP * j, 1),
                    pltpu.roll(w2_end, GROUP * j, 1),
                )
            s2_last = jnp.where(here, s2_end, s2_last)
            w2_last = jnp.where(here, w2_end, w2_last)
            spread = jnp.concatenate(
                [cross[:, LANES:], jnp.zeros((GROUP, LANES - GROUP), F32)], 1
            )
            spread = jnp.where(iota_lane <= iota_row, spread, cross[:, :LANES])
            spread = pltpu.roll(spread, LANES - 1, 1)
            fold = GROUP // 2
            spread = spread[:fold] + pltpu.roll(spread[fold:], LANES - fold, 1)
            while fold > 1:
                fold //= 2
                spread = spread + pltpu.roll(pltpu.roll(spread, 8 - fold, 0), LANES - fold, 1)
            sums[pl.ds(tile, 1), 25 + j : 26 + j, :] = spread[:1][None]
        s2_parts = swap_blocks(s2_parts) + [s2_last]
        w2_parts = swap_blocks(w2_parts) + [w2_last]

        for r in range(0, rows + 2 * GROUP, GROUP):
            sm[r : r + GROUP, :] = mid_in[i, r : r + GROUP, :].astype(F32)
        for r in range(0, rows + GROUP, GROUP):
            sw[r : r + GROUP, :] = k1_in[i, r : r + GROUP, :].astype(F32) * v1_in[
                i, r : r + GROUP, :
            ].astype(F32)
        for scratch, own, before in ((sq, q, pq), (sk, k, pk), (sv, v, pv)):
            scratch[base - EDGE : base, :] = before[:, lanes].astype(F32)
            for r in range(0, rows, GROUP):
                scratch[base + r : base + r + GROUP, :] = own[r : r + GROUP, lanes].astype(F32)
        for r in range(0, rows, GROUP):
            sg[r : r + GROUP, :] = g[r : r + GROUP, lanes].astype(F32)
        sg[rows : rows + EDGE, :] = ng[:, lanes].astype(F32)

        def put(row, x, taps, totals):
            column = x * (channels // LANES) + tile
            to = lax.div(column, 3)
            place = lax.rem(column, 3)
            for n in range(taps):
                sums[pl.ds(to, 1), pl.ds(row + 3 * n + place, 1), :] = jnp.sum(
                    totals[n], axis=0, keepdims=True
                )[None]

        mk, mv = taps_of(fmk, lanes), taps_of(fmv, lanes)
        acc = [[jnp.zeros((GROUP, LANES), F32) for _ in range(3)] for _ in range(3)]
        for a in range(BLOCKS + 1):
            t = a * GROUP
            m = [sm[base + t - j : base + t - j + GROUP, :] for j in range(3)]
            k2 = mk[0] * m[0] + mk[1] * m[1] + mk[2] * m[2]
            v2 = mv[0] * m[0] + mv[1] * m[1] + mv[2] * m[2]
            s2 = s2_parts[a].astype(F32)
            w2 = w2_parts[a].astype(F32)
            parts = (sg[t : t + GROUP, :] * s2, w2 * v2, w2 * k2)
            for x, (ref, value) in enumerate(zip((dq, dk, dv), parts)):
                ref[t : t + GROUP, :] = value
                if a < BLOCKS:
                    for j in range(3):
                        acc[x][j] = acc[x][j] + value * m[j]
        for x in range(3):
            put(9, x, 3, acc[x])
        mq = taps_of(fmq, lanes)
        for a in range(BLOCKS + 1):
            t = a * GROUP
            dmid = (
                sg[t : t + GROUP, :]
                + ahead_taps(mq, dq, t, GROUP)
                + ahead_taps(mk, dk, t, GROUP)
                + ahead_taps(mv, dv, t, GROUP)
            )
            if a < BLOCKS:
                grad_res[t : t + GROUP, lanes] = dmid.astype(BF16)
            d1[t : t + GROUP, :] = dmid * q1_in[i, t : t + GROUP, :].astype(F32)
            eq[t : t + GROUP, :] = dmid * s1_in[i, t : t + GROUP, :].astype(F32)
        ts = taps_of(short, lanes)
        acc = [jnp.zeros((GROUP, LANES), F32) for _ in range(len(ts))]
        for a in range(BLOCKS + 1):
            t = a * GROUP
            dw1 = ahead_taps(ts, d1, t, GROUP)
            ek[t : t + GROUP, :] = dw1 * v1_in[i, base + t : base + t + GROUP, :].astype(F32)
            ev[t : t + GROUP, :] = dw1 * k1_in[i, base + t : base + t + GROUP, :].astype(F32)
            if a < BLOCKS:
                slope = d1[t : t + GROUP, :]
                for n in range(len(ts)):
                    acc[n] = acc[n] + slope * sw[base + t - n : base + t - n + GROUP, :]
        for n in range(len(ts)):
            sums[pl.ds(tile, 1), 18 + n : 19 + n, :] = jnp.sum(acc[n], axis=0, keepdims=True)[None]
        for x, (ref, taps_ref, stream) in enumerate(((eq, fsq, sq), (ek, fsk, sk), (ev, fsv, sv))):
            taps = taps_of(taps_ref, lanes)
            acc = [jnp.zeros((GROUP, LANES), F32) for _ in range(3)]
            for a in range(BLOCKS):
                t = a * GROUP
                e = [ref[t + j : t + j + GROUP, :] for j in range(3)]
                out_buf[slot, x, t : t + GROUP, lanes] = (
                    taps[0] * e[0] + taps[1] * e[1] + taps[2] * e[2]
                ).astype(BF16)
                for j in range(3):
                    acc[j] = acc[j] + e[0] * stream[base + t - j : base + t - j + GROUP, :]
            put(0, x, 3, acc)
        return carry

    lax.fori_loop(0, TILES, one_tile, 0)
    for copy in copies(step, slot):
        copy.start()

    @pl.when(step == steps - 1)
    def _():
        @pl.when(steps > 1)
        def _():
            for copy in copies(step - 1, 1 - slot):
                copy.wait()

        for copy in copies(step, slot):
            copy.wait()


def columns(rows, first=0):
    width = TILES * LANES
    return pl.BlockSpec((rows, width), lambda j: (0, first + j))


def tiled(rows):
    return pl.BlockSpec((TILES, rows, LANES), lambda j: (j, 0, 0))


def shards(
    residual_in, se_streams, cotangent, feat_short, feat_medium, short_filter, medium_filter_weight
):
    res, streams, g = residual_in[0], se_streams[0], cotangent[0]
    rows, channels = res.shape
    seqs, slabs = lax.axis_size("seq"), lax.axis_size("dp")
    tiles = channels // LANES
    steps = tiles // TILES
    groups = medium_filter_weight.shape[1]
    before = shift_rows(
        jnp.concatenate([streams[rows - EDGE :], res[rows - EDGE :]], 1), "seq", 1
    )
    after = shift_rows(
        jnp.concatenate([streams[:EDGE], res[:EDGE], g[:EDGE]], 1), "seq", -1
    )
    edge = functools.partial(columns, EDGE)
    tap_specs = [columns(3, x * steps) for x in range(3)]
    filters = (feat_short,) * 3 + (short_filter,) + (feat_medium,) * 3
    filter_specs = tap_specs + [columns(short_filter.shape[0])] + tap_specs
    long, ext = rows + 2 * GROUP, rows + GROUP
    saved = [long, ext, ext, long, long]
    scratch = pltpu.VMEM((FRAME + ext, LANES), F32)
    w_own, w_edge, d_own, mid, q1, s1, k1, v1 = pl.pallas_call(
        functools.partial(first_kernel, rows),
        grid=(steps,),
        in_specs=[columns(rows, x * steps) for x in range(3)]
        + [columns(rows)] * 2
        + [edge(x * steps) for x in range(4)]
        + [edge(x * steps) for x in range(5)]
        + filter_specs,
        out_specs=[tiled(rows), tiled(GROUP), tiled(ext)] + [tiled(n) for n in saved],
        out_shape=[
            jax.ShapeDtypeStruct((tiles, n, LANES), BF16) for n in [rows, GROUP, ext] + saved
        ],
        scratch_shapes=[scratch] * 7,
        compiler_params=pltpu.CompilerParams(vmem_limit_bytes=48 * 1024 * 1024),
        name="products",
    )(
        *[streams] * 3, res, g, *[before] * 4, *[after] * 5, *filters
    )
    w_prev = shift_rows(w_own, "seq", 1)
    d_next = shift_rows(d_own, "seq", -1)
    taps_fwd = medium_filter_weight.T.astype(F32)
    taps_rev = taps_fwd[:, ::-1]
    per_step = pl.BlockSpec((TILES * BLOCKS, LANES), lambda j: (j, 0))
    row_buf = lambda n: pltpu.VMEM((n, LANES), F32)
    grad_res, grad_streams, sums = pl.pallas_call(
        functools.partial(second_kernel, rows, channels),
        grid=(steps,),
        in_specs=[columns(rows, x * steps) for x in range(3)]
        + [columns(rows)]
        + [edge(x * steps) for x in range(3)]
        + [edge(4 * steps)]
        + [tiled(rows), tiled(GROUP), tiled(rows), tiled(ext), tiled(ext)]
        + [per_step] * 2
        + [tiled(n) for n in saved]
        + filter_specs,
        out_specs=[
            columns(rows),
            pl.BlockSpec(memory_space=pl.ANY),
            pl.BlockSpec((tiles, 40, LANES), lambda j: (0, 0, 0)),
        ],
        out_shape=[
            jax.ShapeDtypeStruct((rows, channels), BF16),
            jax.ShapeDtypeStruct((rows, 3 * channels), BF16),
            jax.ShapeDtypeStruct((tiles, 40, LANES), F32),
        ],
        scratch_shapes=[row_buf(GROUP + rows)] * 3
        + [row_buf(ext), row_buf(long), row_buf(ext)]
        + [row_buf(ext + 8)] * 7
        + [
            pltpu.VMEM((2, 3, rows, TILES * LANES), BF16),
            pltpu.SemaphoreType.DMA((2, 3)),
        ],
        compiler_params=pltpu.CompilerParams(vmem_limit_bytes=48 * 1024 * 1024),
        name="gradients",
    )(
        *[streams] * 3, g, *[before] * 3, after,
        w_own, w_edge, w_prev, d_own, d_next, taps_fwd, taps_rev,
        mid, q1, s1, k1, v1, *filters
    )
    norm_factor = 1.0 / math.sqrt(slabs * seqs * rows)
    parts = lax.all_to_all(sums[:, :33], "seq", split_axis=0, concat_axis=0, tiled=True)
    share = jnp.sum(parts, axis=0) * norm_factor
    others = [
        lax.ppermute(share, "dp", [(i, (i + n) % slabs) for i in range(slabs)])
        for n in range(1, slabs)
    ]
    for other in others:
        share = share + other
    return (
        grad_res[None],
        grad_streams[None],
        share[0:9].reshape(3, -1),
        share[9:18].reshape(3, -1),
        share[18:25],
        share[25:33, ::-1].T,
    )


def solution(mesh):
    placed = (P("dp", "seq", None), P("dp", "seq", None), P("dp", "seq", None), P(), P(), P(), P())
    return jax.shard_map(
        shards,
        mesh=mesh,
        in_specs=placed,
        out_specs=(
            P("dp", "seq", None),
            P("dp", "seq", None),
            P(None, "seq"),
            P(None, "seq"),
            P(None, "seq"),
            P(None, "seq"),
        ),
        check_vma=False,
    )
```

```python
import functools
import math

import jax
import jax.numpy as jnp
from jax import lax
from jax.experimental import pallas as pl
from jax.experimental.pallas import tpu as pltpu
from jax.sharding import PartitionSpec as P

F32 = jnp.float32
BF16 = jnp.bfloat16
LANES = 128
GROUP = 16
GROUPS = LANES // GROUP
SPAN = 32
BLOCKS = LANES // SPAN
JOINED = SPAN // GROUP
EDGE = 10
FRAME = 24
BANDS = 64
TILES = 4


def shift_rows(array, axis, by):
    peers = lax.axis_size(axis)
    return lax.ppermute(array, axis, [(i, i + by) for i in range(peers) if 0 <= i + by < peers])


def lane_blocks(shape):
    return lax.broadcasted_iota(jnp.int32, shape, 1) // SPAN


def swap_blocks(parts):
    parts = list(parts)
    block = lane_blocks(parts[0].shape)
    step = BLOCKS // 2
    while step:
        low = (block & step) == 0
        shift = SPAN * step
        for i in range(BLOCKS):
            if i & step == 0:
                first, second = parts[i], parts[i + step]
                parts[i] = jnp.where(low, first, pltpu.roll(second, shift, 1))
                parts[i + step] = jnp.where(low, pltpu.roll(first, LANES - shift, 1), second)
        step //= 2
    return parts


def taps_of(ref, lanes):
    return [ref[i : i + 1, lanes] for i in range(ref.shape[0])]


def back_taps(taps, ref, start, rows):
    total = taps[0] * ref[start : start + rows, :]
    for i in range(1, len(taps)):
        total = total + taps[i] * ref[start - i : start - i + rows, :]
    return total


def ahead_taps(taps, ref, start, rows):
    total = taps[0] * ref[start : start + rows, :]
    for i in range(1, len(taps)):
        total = total + taps[i] * ref[start + i : start + i + rows, :]
    return total


def first_kernel(rows, *refs):
    (q, k, v, res, g, pq, pk, pv, pr, nq, nk, nv, nr, ng) = refs[:14]
    (fsq, fsk, fsv, short, fmq, fmk, fmv) = refs[14:21]
    (w_own, w_edge, d_own, mid_out, q1_out, s1_out, k1_out, v1_out) = refs[21:29]
    (sq, sk, sv, sr, sg, sw, sm) = refs[29:]
    total = rows + GROUP

    @pl.when(pl.program_id(0) == 0)
    def _():
        for ref in (sq, sk, sv, sr, sg):
            ref[...] = jnp.zeros(ref.shape, F32)

    def one_tile(i, carry):
        lanes = pl.ds(pl.multiple_of(i * LANES, LANES), LANES)
        for scratch, own, before, after in (
            (sq, q, pq, nq),
            (sk, k, pk, nk),
            (sv, v, pv, nv),
            (sr, res, pr, nr),
            (sg, g, None, ng),
        ):
            if before is not None:
                scratch[FRAME - EDGE : FRAME, :] = before[:, lanes].astype(F32)
            for r in range(0, rows, GROUP):
                scratch[FRAME + r : FRAME + r + GROUP, :] = own[r : r + GROUP, lanes].astype(F32)
            scratch[FRAME + rows : FRAME + rows + EDGE, :] = after[:, lanes].astype(F32)
        tq, tk, tv = taps_of(fsq, lanes), taps_of(fsk, lanes), taps_of(fsv, lanes)
        for t in range(-GROUP, total, GROUP):
            at = FRAME + t
            k1 = back_taps(tk, sk, at, GROUP)
            v1 = back_taps(tv, sv, at, GROUP)
            sw[at : at + GROUP, :] = k1 * v1
            k1_out[i, t + GROUP : t + 2 * GROUP, :] = k1.astype(BF16)
            v1_out[i, t + GROUP : t + 2 * GROUP, :] = v1.astype(BF16)
        ts = taps_of(short, lanes)
        for t in range(-GROUP, total, GROUP):
            at = FRAME + t
            q1 = back_taps(tq, sq, at, GROUP)
            s1 = back_taps(ts, sw, at, GROUP)
            mid = (sr[at : at + GROUP, :] + q1 * s1).astype(BF16)
            sm[at : at + GROUP, :] = mid.astype(F32)
            mid_out[i, t + GROUP : t + 2 * GROUP, :] = mid
            if t >= 0:
                q1_out[i, t : t + GROUP, :] = q1.astype(BF16)
                s1_out[i, t : t + GROUP, :] = s1.astype(BF16)
        mq, mk, mv = taps_of(fmq, lanes), taps_of(fmk, lanes), taps_of(fmv, lanes)
        products, slopes = [], []
        for t in range(0, total, GROUP):
            at = FRAME + t
            m = [sm[at - j : at - j + GROUP, :] for j in range(3)]
            q2, k2, v2 = [
                taps[0] * m[0] + taps[1] * m[1] + taps[2] * m[2] for taps in (mq, mk, mv)
            ]
            products.append((k2 * v2).astype(BF16))
            slopes.append((sg[at : at + GROUP, :] * q2).astype(BF16))
        for values, own in ((products, w_own), (slopes, d_own)):
            parts = [
                jnp.concatenate(values[j : j + JOINED], 0)
                for j in range(0, GROUPS, JOINED)
            ]
            for j, part in enumerate(swap_blocks(parts)):
                own[i, j * SPAN : (j + 1) * SPAN, :] = part
        w_edge[i] = products[GROUPS]
        d_own[i, rows : rows + GROUP, :] = slopes[GROUPS]
        return carry

    lax.fori_loop(0, TILES, one_tile, 0)


def windows(low, high, last, block):
    rows = []
    for k in range(BLOCKS + 1):
        if k == 0:
            first, second = low, high
        elif k == BLOCKS:
            first, second = high, last
        else:
            shift = LANES - SPAN * k
            second = pltpu.roll(high, shift, 1)
            first = jnp.where(block < BLOCKS - k, pltpu.roll(low, shift, 1), second)
        rows.append(jnp.concatenate([first, second], 1))
    return jnp.concatenate(rows, 0)


def fold_diagonals(parts):
    row = lax.broadcasted_iota(jnp.int32, parts[0].shape, 0)
    half = len(parts) // 2
    while half:
        first = (row & half) == 0
        folded = []
        for x, y in zip(parts[:half], parts[half:]):
            low = jnp.where(first, x, pltpu.roll(y, half, 0))
            high = jnp.where(first, pltpu.roll(x, 8 - half, 0), y)
            folded.append(low + pltpu.roll(high, LANES - half, 1))
        parts = folded
        half //= 2
    return parts[0]


def fold_rows(parts):
    row = lax.broadcasted_iota(jnp.int32, parts[0].shape, 0)
    half = len(parts) // 2
    while half:
        first = (row & half) == 0
        parts = [
            jnp.where(first, x, pltpu.roll(y, half, 0))
            + jnp.where(first, pltpu.roll(x, 8 - half, 0), y)
            for x, y in zip(parts[:half], parts[half:])
        ]
        half //= 2
    return parts[0]


def toeplitz_kernel(taps_fwd, taps_rev, lag_out, ahead_out):
    shape = (SPAN, LANES)
    for j in range(BANDS):
        part = slice(j * SPAN, (j + 1) * SPAN)
        for taps, first, out in ((taps_fwd, 0, ahead_out), (taps_rev, 1, lag_out)):
            turned = pltpu.roll(
                jnp.broadcast_to(taps[j : j + 1, :], shape), first, 1, stride=1, stride_axis=0
            )
            out[part, :] = turned.astype(BF16)


def second_kernel(rows, channels, *refs):
    (q, k, v, g, pq, pk, pv, ng) = refs[:8]
    (w_own, w_edge, w_prev, d_own, d_next, lag_in, ahead_in) = refs[8:15]
    (mid_in, q1_in, s1_in, k1_in, v1_in) = refs[15:20]
    (fsq, fsk, fsv, short, fmq, fmk, fmv) = refs[20:27]
    (grad_res, grad_streams, sums_out) = refs[27:30]
    (sq, sk, sv, sg, sm, sw, dq, dk, dv, d1, eq, ek, ev) = refs[30:43]
    (s2_apart, w2_apart, s2_ends, w2_ends, s2_nat, w2_nat, diagonals, wins, d_wins) = refs[43:52]
    (s2_raw, w2_raw, acc, sums, moved, out_buf, sems) = refs[52:]
    now = pl.program_id(0)
    steps = pl.num_programs(0) - 1
    step = now - 1
    slot = lax.rem(now + 1, 2)
    width = TILES * LANES
    base = GROUP
    block = lane_blocks((SPAN, LANES))
    zero = jnp.zeros((), BF16)

    def copies(at_step, at_slot):
        return [
            pltpu.make_async_copy(
                out_buf.at[at_slot, x],
                grad_streams.at[
                    :, pl.ds(pl.multiple_of(x * channels + at_step * width, width), width)
                ],
                sems.at[at_slot, x],
            )
            for x in range(3)
        ]

    def lanes_of(i):
        return pl.ds(pl.multiple_of(i * LANES, LANES), LANES)

    def slot_of(n):
        return lax.broadcasted_iota(jnp.int32, (n, LANES), 1) // GROUP % JOINED

    def pick(wide, count, lanes):
        out = wide[:count, lanes]
        for n in range(1, JOINED):
            out = jnp.where(slot_of(count) == n, wide[n * SPAN : n * SPAN + count, lanes], out)
        return out

    def window_stage(i, j):
        part = slice(j * SPAN, (j + 1) * SPAN)
        no_rows = jnp.zeros((SPAN - GROUP, LANES), BF16)
        last_w = w_edge[i]
        last_d = d_next[i, rows : rows + GROUP, :]
        if j:
            last_w = pltpu.roll(last_w, LANES - SPAN * j, 1)
            last_d = pltpu.roll(last_d, LANES - SPAN * j, 1)
        for low, high, last, out in (
            (w_prev[i, part, :], w_own[i, part, :], last_w, wins),
            (d_own[i, part, :], d_next[i, part, :], last_d, d_wins),
        ):
            win = windows(low, high, jnp.concatenate([last, no_rows], 0), block)
            for n in range(2):
                out[n, :, j * LANES : (j + 1) * LANES] = win[:, n * LANES : (n + 1) * LANES]

    def filter_stage(i, j):
        taps_part = pl.ds((i * BLOCKS + j) * JOINED * SPAN, JOINED * SPAN)
        row = lax.broadcasted_iota(jnp.int32, (JOINED * SPAN, LANES), 0) % SPAN
        lane = lax.broadcasted_iota(jnp.int32, (JOINED * SPAN, LANES), 1)
        for bands, inside, win, raw in (
            (lag_in, lane > row, wins, s2_raw),
            (ahead_in, lane >= row, d_wins, w2_raw),
        ):
            at = slice(j * LANES, (j + 1) * LANES)
            turned = bands[taps_part, :]
            over = jnp.where(inside, zero, turned)[:, :SPAN]
            raw[j % 2] = jnp.dot(
                jnp.concatenate([jnp.where(inside, turned, zero), over], 1),
                jnp.concatenate([win[0, :, at], win[1, :, at]], 1),
                preferred_element_type=F32,
            )

    def pick_stage(j):
        part = slice(j * SPAN, (j + 1) * SPAN)
        main, edge = slice(0, LANES), slice(LANES, 2 * LANES)
        for raw, apart_ref, ends_ref in ((s2_raw, s2_apart, s2_ends), (w2_raw, w2_apart, w2_ends)):
            value = raw[j % 2].astype(BF16)
            apart_ref[part, :] = pick(value, SPAN, main)
            end = pick(value, GROUP, edge)
            ends_ref[j] = pltpu.roll(end, SPAN * j, 1) if j else end

    def cross_stage(i, first):
        row = lax.broadcasted_iota(jnp.int32, (SPAN, LANES), 0)
        lane = lax.broadcasted_iota(jnp.int32, (SPAN, LANES), 1)
        nothing = jnp.zeros((SPAN, LANES), BF16)
        apart = []
        for j in (first, first + 1):
            own_d = d_own[i, j * SPAN : (j + 1) * SPAN, :]
            for n in range(JOINED):
                mine = jnp.where(slot_of(SPAN) == n, own_d, zero)
                pair = [mine, nothing] if j == first else [nothing, mine]
                apart.append(jnp.concatenate(pair, 1))
        cross = lax.dot_general(
            jnp.concatenate(apart, 0),
            wins[0, :, first * LANES : (first + 2) * LANES],
            (((1,), (1,)), ((), ())),
            preferred_element_type=F32,
        )
        for n in range(2 * JOINED):
            mine = cross[n * SPAN : (n + 1) * SPAN]
            over = jnp.concatenate(
                [mine[:, LANES:], jnp.zeros((SPAN, LANES - SPAN), F32)], 1
            )
            mine = jnp.where(lane <= row, over, mine[:, :LANES])
            diagonals[first * JOINED + n] = sum(
                pltpu.roll(mine[r : r + 8], LANES - 1 - r, 1) for r in range(0, SPAN, 8)
            )

    def natural_stage(f):
        place = lax.rem(f + 2 * TILES, 2 * TILES)
        for apart_ref, ends_ref, nat in ((s2_apart, s2_ends, s2_nat), (w2_apart, w2_ends, w2_nat)):
            parts = swap_blocks([apart_ref[j * SPAN : (j + 1) * SPAN, :] for j in range(BLOCKS)])
            for j in range(BLOCKS):
                nat[place, j * SPAN : (j + 1) * SPAN, :] = parts[j]
            end = ends_ref[0]
            for j in range(1, BLOCKS):
                end = jnp.where(lane_blocks((GROUP, LANES)) == j, ends_ref[j], end)
            nat[place, rows : rows + GROUP, :] = end

    def fold_stage(f):
        sums[pl.ds(jnp.maximum(f, 0), 1), :GROUPS, :] = fold_diagonals(
            [diagonals[j] for j in range(GROUPS)]
        )[None]

    def input_stage(i):
        lanes = lanes_of(i)
        par = lax.rem(i, 2)
        for r in range(0, rows + 2 * GROUP, GROUP):
            sm[par, r : r + GROUP, :] = mid_in[i, r : r + GROUP, :].astype(F32)
        for r in range(0, rows + GROUP, GROUP):
            sw[par, r : r + GROUP, :] = k1_in[i, r : r + GROUP, :].astype(F32) * v1_in[
                i, r : r + GROUP, :
            ].astype(F32)
        for scratch, own, before in ((sq, q, pq), (sk, k, pk), (sv, v, pv)):
            scratch[par, base - EDGE : base, :] = before[:, lanes].astype(F32)
            for r in range(0, rows, GROUP):
                scratch[par, base + r : base + r + GROUP, :] = own[r : r + GROUP, lanes].astype(F32)
        sg[0:EDGE, :] = ng[:, lanes].astype(F32)

    def add_up(first, values, others, fresh):
        for n, other in enumerate(others):
            total = None
            for x, y in zip(values, other):
                product = x * y
                for r in range(0, GROUP, 8):
                    half = product[r : r + 8]
                    total = half if total is None else total + half
            acc[first + n] = total if fresh else acc[first + n] + total

    def element_stage(i, chunks):
        lanes = lanes_of(i)
        par = lax.rem(i, 2)
        place = lax.rem(step * TILES + i + 2 * TILES, 2 * TILES)
        main = chunks[0] < GROUPS
        fresh = chunks[0] == GROUPS - 1
        mq, mk, mv = taps_of(fmq, lanes), taps_of(fmk, lanes), taps_of(fmv, lanes)
        starts = [a * GROUP for a in chunks]
        at = lambda ref, t: ref[t : t + GROUP, :]
        gs = [g[t : t + GROUP, lanes].astype(F32) if main else sg[...] for t in starts]
        tall = lambda ref, t: ref[par, t : t + GROUP, :]
        mids = [[tall(sm, base + t - n) for t in starts] for n in range(3)]
        parts = [[], [], []]
        for c, t in enumerate(starts):
            m = [mids[n][c] for n in range(3)]
            k2 = mk[0] * m[0] + mk[1] * m[1] + mk[2] * m[2]
            v2 = mv[0] * m[0] + mv[1] * m[1] + mv[2] * m[2]
            s2 = s2_nat[place, t : t + GROUP, :].astype(F32)
            w2 = w2_nat[place, t : t + GROUP, :].astype(F32)
            for x, (ref, value) in enumerate(
                zip((dq, dk, dv), (gs[c] * s2, w2 * v2, w2 * k2))
            ):
                ref[t : t + GROUP, :] = value
                parts[x].append(value)
        if main:
            for x in range(3):
                add_up(9 + 3 * x, parts[x], mids, fresh)
        slopes = []
        for c, t in enumerate(starts):
            dmid = (
                gs[c]
                + ahead_taps(mq, dq, t, GROUP)
                + ahead_taps(mk, dk, t, GROUP)
                + ahead_taps(mv, dv, t, GROUP)
            )
            if main:
                grad_res[t : t + GROUP, lanes] = dmid.astype(BF16)
            slope = dmid * q1_in[i, t : t + GROUP, :].astype(F32)
            d1[t : t + GROUP, :] = slope
            slopes.append(slope)
            eq[t : t + GROUP, :] = dmid * s1_in[i, t : t + GROUP, :].astype(F32)
        ts = taps_of(short, lanes)
        if main:
            lagged = [[tall(sw, base + t - n) for t in starts] for n in range(len(ts))]
            add_up(18, slopes, lagged, fresh)
        for t in starts:
            dw1 = ahead_taps(ts, d1, t, GROUP)
            ek[t : t + GROUP, :] = dw1 * v1_in[i, base + t : base + t + GROUP, :].astype(F32)
            ev[t : t + GROUP, :] = dw1 * k1_in[i, base + t : base + t + GROUP, :].astype(F32)
        if not main:
            return
        for x, (ref, taps_ref, stream) in enumerate(((eq, fsq, sq), (ek, fsk, sk), (ev, fsv, sv))):
            taps = taps_of(taps_ref, lanes)
            for t in starts:
                out_buf[slot, x, t : t + GROUP, lanes] = ahead_taps(taps, ref, t, GROUP).astype(
                    BF16
                )
            add_up(
                3 * x,
                [at(ref, t) for t in starts],
                [[tall(stream, base + t - n) for t in starts] for n in range(3)],
                fresh,
            )

    def totals_stage(i):
        tile = pl.ds(jnp.maximum(step * TILES + i, 0), 1)
        for n in range(0, 24, 8):
            sums[tile, GROUPS + n : GROUPS + n + 8, :] = fold_rows(
                [acc[n + j] for j in range(8)]
            )[None]
        sums[tile, 32:33, :] = jnp.sum(acc[24], axis=0, keepdims=True)[None]

    @pl.when(now == 0)
    def _():
        for ref in (sg, dq, dk, dv, d1, eq, ek, ev):
            ref[...] = jnp.zeros(ref.shape, F32)

    @pl.when(step >= 2)
    def _():
        for copy in copies(step - 2, slot):
            copy.wait()

    def one_tile(filtering, differentiating):
        def run(i, carry):
            flat = now * TILES + i
            for j in reversed(range(BLOCKS)):

                @pl.when(i >= 0)
                def _():
                    if filtering:
                        if j == 3:
                            fold_stage(flat - 1)
                            pick_stage(0)
                        else:
                            if j == 2:
                                natural_stage(flat - 1)
                            pick_stage(j + 1)
                        filter_stage(i, j)
                        if j == 2:
                            cross_stage(i, 2)
                        if j == 0:
                            cross_stage(i, 0)
                        if j:
                            window_stage(i, j - 1)
                        else:
                            window_stage(jnp.minimum(i + 1, TILES - 1), BLOCKS - 1)
                    if differentiating:
                        element_stage(i, list(reversed(range(j * JOINED, (j + 1) * JOINED))))
                        if j == 1:
                            following = jnp.minimum(i + 1, TILES - 1)
                            input_stage(following)
                            element_stage(following, [GROUPS])
                        if j == 0:
                            totals_stage(i)

            return carry

        return run

    @pl.when(now == 0)
    def _():
        window_stage(0, BLOCKS - 1)
        lax.fori_loop(0, TILES, one_tile(True, False), 0)

    @pl.when(jnp.logical_and(now > 0, now < steps))
    def _():
        window_stage(0, BLOCKS - 1)
        input_stage(0)
        element_stage(0, [GROUPS])
        lax.fori_loop(0, TILES, one_tile(True, True), 0)

    @pl.when(now == steps)
    def _():
        fold_stage(now * TILES - 1)
        pick_stage(0)
        natural_stage(now * TILES - 1)
        input_stage(0)
        element_stage(0, [GROUPS])
        lax.fori_loop(0, TILES, one_tile(False, True), 0)

    @pl.when(step >= 0)
    def _():
        for copy in copies(step, slot):
            copy.start()

    @pl.when(now == steps)
    def _():
        tiles = sums.shape[0]
        for x in range(3):
            for tile in range(tiles):
                to, place = divmod(x * tiles + tile, 3)
                for n in range(3):
                    for row in (GROUPS, GROUPS + 9):
                        moved[to, row + 3 * n + place : row + 3 * n + place + 1, :] = sums[
                            tile, row + 3 * x + n : row + 3 * x + n + 1, :
                        ]
        for tile in range(tiles):
            moved[tile, :GROUPS, :] = sums[tile, :GROUPS, :]
            moved[tile, 26:33, :] = sums[tile, 26:33, :]
        sums_out[...] = moved[:, :33, :].astype(BF16)

        @pl.when(steps > 1)
        def _():
            for copy in copies(step - 1, 1 - slot):
                copy.wait()

        for copy in copies(step, slot):
            copy.wait()


def last_kernel(scale, first, second, third, fourth, fs_out, fm_out, short_out, medium_out):
    total = (first[...] + second[...] + third[...] + fourth[...]) * scale
    for out, row in ((fs_out, 8), (fm_out, 17)):
        for n in range(9):
            lanes = slice(n % 3 * LANES, (n % 3 + 1) * LANES)
            out[n // 3 : n // 3 + 1, lanes] = total[row + n : row + n + 1]
    short_out[...] = total[26:33]
    row = lax.broadcasted_iota(jnp.int32, (LANES, LANES), 0)
    lane = lax.broadcasted_iota(jnp.int32, (LANES, LANES), 1)
    flip = jnp.where(row + lane == LANES - 1, 1.0, 0.0).astype(F32)
    medium_out[...] = lax.dot_general(
        total[0:8],
        flip,
        (((1,), (1,)), ((), ())),
        precision=lax.Precision.HIGHEST,
        preferred_element_type=F32,
    )


def columns(rows, first=0):
    width = TILES * LANES
    return pl.BlockSpec((rows, width), lambda j: (0, first + j))


def moved_spec(spec, move):
    return pl.BlockSpec(spec.block_shape, lambda j: spec.index_map(move(j)))


def tiled(rows):
    return pl.BlockSpec((TILES, rows, LANES), lambda j: (j, 0, 0))


def shards(
    residual_in, se_streams, cotangent, feat_short, feat_medium, short_filter, medium_filter_weight
):
    res, streams, g = residual_in[0], se_streams[0], cotangent[0]
    rows, channels = res.shape
    seqs, slabs = lax.axis_size("seq"), lax.axis_size("dp")
    tiles = channels // LANES
    steps = tiles // TILES
    groups = medium_filter_weight.shape[1]
    before = shift_rows(
        jnp.concatenate([streams[rows - EDGE :], res[rows - EDGE :]], 1), "seq", 1
    )
    after = shift_rows(
        jnp.concatenate([streams[:EDGE], res[:EDGE], g[:EDGE]], 1), "seq", -1
    )
    edge = functools.partial(columns, EDGE)
    tap_specs = [columns(3, x * steps) for x in range(3)]
    filters = (feat_short,) * 3 + (short_filter,) + (feat_medium,) * 3
    filter_specs = tap_specs + [columns(short_filter.shape[0])] + tap_specs
    long, ext = rows + 2 * GROUP, rows + GROUP
    saved = [long, ext, ext, long, long]
    scratch = pltpu.VMEM((FRAME + ext, LANES), F32)
    w_own, w_edge, d_own, mid, q1, s1, k1, v1 = pl.pallas_call(
        functools.partial(first_kernel, rows),
        grid=(steps,),
        in_specs=[columns(rows, x * steps) for x in range(3)]
        + [columns(rows)] * 2
        + [edge(x * steps) for x in range(4)]
        + [edge(x * steps) for x in range(5)]
        + filter_specs,
        out_specs=[tiled(rows), tiled(GROUP), tiled(ext)] + [tiled(n) for n in saved],
        out_shape=[
            jax.ShapeDtypeStruct((tiles, n, LANES), BF16) for n in [rows, GROUP, ext] + saved
        ],
        scratch_shapes=[scratch] * 7,
        compiler_params=pltpu.CompilerParams(vmem_limit_bytes=48 * 1024 * 1024),
        name="products",
    )(
        *[streams] * 3, res, g, *[before] * 4, *[after] * 5, *filters
    )
    w_prev = shift_rows(w_own, "seq", 1)
    d_next = shift_rows(d_own, "seq", -1)
    taps_fwd = medium_filter_weight.T.astype(F32)
    taps_rev = taps_fwd[:, ::-1]
    bands = pl.BlockSpec((BANDS * SPAN, LANES), lambda j: (j, 0))
    lag, ahead = pl.pallas_call(
        toeplitz_kernel,
        grid=(groups // BANDS,),
        in_specs=[pl.BlockSpec((BANDS, LANES), lambda j: (j, 0))] * 2,
        out_specs=[bands] * 2,
        out_shape=[jax.ShapeDtypeStruct((groups * SPAN, LANES), BF16)] * 2,
        name="toeplitz",
    )(taps_fwd, taps_rev)
    per_step = pl.BlockSpec((TILES * GROUPS * SPAN, LANES), lambda j: (j, 0))
    row_buf = lambda n: pltpu.VMEM((n, LANES), F32)
    element_specs = (
        [columns(rows, x * steps) for x in range(3)]
        + [columns(rows)]
        + [edge(x * steps) for x in range(3)]
        + [edge(4 * steps)]
    )
    behind = lambda spec: moved_spec(spec, lambda j: jnp.maximum(j - 1, 0))
    ahead_of = lambda spec: moved_spec(spec, lambda j: jnp.minimum(j, steps - 1))
    grad_res, grad_streams, sums = pl.pallas_call(
        functools.partial(second_kernel, rows, channels),
        grid=(steps + 1,),
        in_specs=[behind(spec) for spec in element_specs]
        + [
            ahead_of(spec)
            for spec in [tiled(rows), tiled(GROUP), tiled(rows), tiled(ext), tiled(ext)]
            + [per_step] * 2
        ]
        + [behind(spec) for spec in [tiled(n) for n in saved] + filter_specs],
        out_specs=[
            behind(columns(rows)),
            pl.BlockSpec(memory_space=pl.ANY),
            pl.BlockSpec((tiles, 33, LANES), lambda j: (0, 0, 0)),
        ],
        out_shape=[
            jax.ShapeDtypeStruct((rows, channels), BF16),
            jax.ShapeDtypeStruct((rows, 3 * channels), BF16),
            jax.ShapeDtypeStruct((tiles, 33, LANES), BF16),
        ],
        scratch_shapes=[pltpu.VMEM((2, GROUP + rows, LANES), F32)] * 3
        + [row_buf(GROUP)] + [pltpu.VMEM((2, n, LANES), F32) for n in (long, ext)]
        + [row_buf(ext + 8)] * 7
        + [pltpu.VMEM((rows, LANES), BF16)] * 2
        + [pltpu.VMEM((BLOCKS, GROUP, LANES), BF16)] * 2
        + [pltpu.VMEM((2 * TILES, ext, LANES), BF16)] * 2
        + [pltpu.VMEM((GROUPS, 8, LANES), F32)]
        + [pltpu.VMEM((2, LANES + SPAN, BLOCKS * LANES), BF16)] * 2
        + [pltpu.VMEM((2, JOINED * SPAN, 2 * LANES), F32)] * 2
        + [
            pltpu.VMEM((25, 8, LANES), F32),
            pltpu.VMEM((tiles, 40, LANES), F32),
            pltpu.VMEM((tiles, 40, LANES), F32),
            pltpu.VMEM((2, 3, rows, TILES * LANES), BF16),
            pltpu.SemaphoreType.DMA((2, 3)),
        ],
        compiler_params=pltpu.CompilerParams(vmem_limit_bytes=48 * 1024 * 1024),
        name="gradients",
    )(
        *[streams] * 3, g, *[before] * 3, after,
        w_own, w_edge, w_prev, d_own, d_next, lag, ahead,
        mid, q1, s1, k1, v1, *filters
    )
    norm_factor = 1.0 / math.sqrt(slabs * seqs * rows)
    parts = lax.all_to_all(sums, "seq", split_axis=0, concat_axis=0, tiled=True)
    share = jnp.sum(parts.astype(F32), axis=0)
    others = [
        lax.ppermute(share, "dp", [(i, (i + n) % slabs) for i in range(slabs)])
        for n in range(1, slabs)
    ]
    cols = 3 * channels // tiles
    filter_grads = pl.pallas_call(
        functools.partial(last_kernel, norm_factor),
        out_shape=[
            jax.ShapeDtypeStruct(shape, F32)
            for shape in ((3, cols), (3, cols), (7, LANES), (GROUPS, LANES))
        ],
        name="totals",
    )(share, *others)
    return (grad_res[None], grad_streams[None], *filter_grads[:3], filter_grads[3].T)


def solution(mesh):
    placed = (P("dp", "seq", None), P("dp", "seq", None), P("dp", "seq", None), P(), P(), P(), P())
    return jax.shard_map(
        shards,
        mesh=mesh,
        in_specs=placed,
        out_specs=(
            P("dp", "seq", None),
            P("dp", "seq", None),
            P(None, "seq"),
            P(None, "seq"),
            P(None, "seq"),
            P(None, "seq"),
        ),
        check_vma=False,
    )
```

```python
import functools
import math

import jax
import jax.numpy as jnp
from jax import lax
from jax.experimental import pallas as pl
from jax.experimental.pallas import tpu as pltpu
from jax.sharding import PartitionSpec as P

F32 = jnp.float32
BF16 = jnp.bfloat16
LANES = 128
GROUP = 16
GROUPS = LANES // GROUP
SPAN = 32
BLOCKS = LANES // SPAN
JOINED = SPAN // GROUP
EDGE = 10
EARLIER_ROWS = ((20, 4), (0, 10), (10, 10), (24, 2))
EARLIER = 26
LATER = 5 * EDGE
LATER_AT = 32
FRAME = 24
HALVES = 1
TILES = 4


def turn(array, axis, by):
    peers = lax.axis_size(axis)
    return lax.ppermute(array, axis, [(i, (i + by) % peers) for i in range(peers)])


def lane_blocks(shape):
    return lax.broadcasted_iota(jnp.int32, shape, 1) // SPAN


def swap_blocks(parts):
    parts = list(parts)
    block = lane_blocks(parts[0].shape)
    step = BLOCKS // 2
    while step:
        low = (block & step) == 0
        shift = SPAN * step
        for i in range(BLOCKS):
            if i & step == 0:
                first, second = parts[i], parts[i + step]
                parts[i] = jnp.where(low, first, pltpu.roll(second, shift, 1))
                parts[i + step] = jnp.where(low, pltpu.roll(first, LANES - shift, 1), second)
        step //= 2
    return parts


def taps_of(ref, lanes):
    return [ref[i : i + 1, lanes] for i in range(ref.shape[0])]


def back_taps(taps, ref, start, rows):
    total = taps[0] * ref[start : start + rows, :]
    for i in range(1, len(taps)):
        total = total + taps[i] * ref[start - i : start - i + rows, :]
    return total


def ahead_taps(taps, ref, start, rows):
    total = taps[0] * ref[start : start + rows, :]
    for i in range(1, len(taps)):
        total = total + taps[i] * ref[start + i : start + i + rows, :]
    return total


def rim_kernel(lq, lk, lv, lr, fq, fk, fv, fr, fg, before, after, rim):
    for c in range(0, before.shape[1], LANES):
        lanes = slice(c, c + LANES)
        for at, ref in ((16, lr), (14, lq), (10, lv), (0, lk)):
            rim[at : at + GROUP, :] = ref[:, lanes].astype(F32)
        before[:, lanes] = rim[GROUP - EDGE : GROUP - EDGE + EARLIER, :].astype(BF16)
        for x, ref in enumerate((fq, fk, fv, fr, fg)):
            at = LATER_AT + EDGE * x
            rim[at : at + GROUP, :] = ref[:, lanes].astype(F32)
        after[:, lanes] = rim[LATER_AT : LATER_AT + LATER, :].astype(BF16)


def first_kernel(rows, *refs):
    (q, k, v, res, g, before, after) = refs[:7]
    (fsq, fsk, fsv, short, fmq, fmk, fmv, inner) = refs[7:15]
    (w_own, w_edge, d_own, mid_out, q1_out, s1_out, k1_out, v1_out) = refs[15:23]
    (sq, sk, sv, sr, sg, sw, sm, rim) = refs[23:]
    total = rows + GROUP

    @pl.when(pl.program_id(0) == 0)
    def _():
        for ref in (sq, sk, sv, sr, sg):
            ref[...] = jnp.zeros(ref.shape, F32)

    def one_tile(i, carry):
        lanes = pl.ds(pl.multiple_of(i * LANES, LANES), LANES)
        rim[0:EARLIER, :] = before[:, lanes].astype(F32) * inner[0]
        rim[LATER_AT : LATER_AT + LATER, :] = after[:, lanes].astype(F32) * inner[1]
        for x, (scratch, own) in enumerate(((sq, q), (sk, k), (sv, v), (sr, res), (sg, g))):
            if x < 4:
                at, count = EARLIER_ROWS[x]
                scratch[FRAME - count : FRAME, :] = rim[at : at + count, :]
            for r in range(0, rows, GROUP):
                scratch[FRAME + r : FRAME + r + GROUP, :] = own[r : r + GROUP, lanes].astype(F32)
            at = LATER_AT + EDGE * x
            scratch[FRAME + rows : FRAME + rows + EDGE, :] = rim[at : at + EDGE, :]
        tq, tk, tv = taps_of(fsq, lanes), taps_of(fsk, lanes), taps_of(fsv, lanes)
        for t in range(-GROUP, total, GROUP):
            at = FRAME + t
            k1 = back_taps(tk, sk, at, GROUP)
            v1 = back_taps(tv, sv, at, GROUP)
            sw[at : at + GROUP, :] = k1 * v1
            k1_out[i, t + GROUP : t + 2 * GROUP, :] = k1.astype(BF16)
            v1_out[i, t + GROUP : t + 2 * GROUP, :] = v1.astype(BF16)
        ts = taps_of(short, lanes)
        for t in range(-GROUP, total, GROUP):
            at = FRAME + t
            q1 = back_taps(tq, sq, at, GROUP)
            s1 = back_taps(ts, sw, at, GROUP)
            mid = (sr[at : at + GROUP, :] + q1 * s1).astype(BF16)
            sm[at : at + GROUP, :] = mid.astype(F32)
            mid_out[i, t + GROUP : t + 2 * GROUP, :] = mid
            if t >= 0:
                q1_out[i, t : t + GROUP, :] = q1.astype(BF16)
                s1_out[i, t : t + GROUP, :] = s1.astype(BF16)
        mq, mk, mv = taps_of(fmq, lanes), taps_of(fmk, lanes), taps_of(fmv, lanes)
        products, slopes = [], []
        for t in range(0, total, GROUP):
            at = FRAME + t
            m = [sm[at - j : at - j + GROUP, :] for j in range(3)]
            q2, k2, v2 = [
                taps[0] * m[0] + taps[1] * m[1] + taps[2] * m[2] for taps in (mq, mk, mv)
            ]
            products.append((k2 * v2).astype(BF16))
            slopes.append((sg[at : at + GROUP, :] * q2).astype(BF16))
        for values, own in ((products, w_own), (slopes, d_own)):
            parts = [
                jnp.concatenate(values[j : j + JOINED], 0)
                for j in range(0, GROUPS, JOINED)
            ]
            for j, part in enumerate(swap_blocks(parts)):
                own[i, j * SPAN : (j + 1) * SPAN, :] = part
        w_edge[i] = products[GROUPS]
        d_own[i, rows : rows + GROUP, :] = slopes[GROUPS]
        return carry

    lax.fori_loop(0, TILES, one_tile, 0)


def windows(low, high, last, block):
    rows = []
    for k in range(BLOCKS + 1):
        if k == 0:
            first, second = low, high
        elif k == BLOCKS:
            first, second = high, last
        else:
            shift = LANES - SPAN * k
            second = pltpu.roll(high, shift, 1)
            first = jnp.where(block < BLOCKS - k, pltpu.roll(low, shift, 1), second)
        rows.append(jnp.concatenate([first, second], 1))
    return jnp.concatenate(rows, 0)


def fold_diagonals(parts):
    row = lax.broadcasted_iota(jnp.int32, parts[0].shape, 0)
    half = len(parts) // 2
    while half:
        first = (row & half) == 0
        folded = []
        for x, y in zip(parts[:half], parts[half:]):
            low = jnp.where(first, x, pltpu.roll(y, half, 0))
            high = jnp.where(first, pltpu.roll(x, 8 - half, 0), y)
            folded.append(low + pltpu.roll(high, LANES - half, 1))
        parts = folded
        half //= 2
    return parts[0]


def fold_rows(parts):
    row = lax.broadcasted_iota(jnp.int32, parts[0].shape, 0)
    half = len(parts) // 2
    while half:
        first = (row & half) == 0
        parts = [
            jnp.where(first, x, pltpu.roll(y, half, 0))
            + jnp.where(first, pltpu.roll(x, 8 - half, 0), y)
            for x, y in zip(parts[:half], parts[half:])
        ]
        half //= 2
    return parts[0]


def toeplitz_kernel(taps, lag_out, ahead_out, taps_fwd, taps_rev):
    row = lax.broadcasted_iota(jnp.int32, (LANES, LANES), 0)
    lane = lax.broadcasted_iota(jnp.int32, (LANES, LANES), 1)
    for out, places in ((taps_fwd, row == lane), (taps_rev, row + lane == LANES - 1)):
        out[...] = lax.dot_general(
            taps[...],
            jnp.where(places, 1.0, 0.0).astype(BF16),
            (((0,), (0,)), ((), ())),
            preferred_element_type=F32,
        )
    shape = (SPAN, LANES)
    for j in range(LANES):
        part = slice(j * SPAN, (j + 1) * SPAN)
        for taps, first, out in ((taps_fwd, 0, ahead_out), (taps_rev, 1, lag_out)):
            turned = pltpu.roll(
                jnp.broadcast_to(taps[j : j + 1, :], shape), first, 1, stride=1, stride_axis=0
            )
            out[part, :] = turned.astype(BF16)


def second_kernel(rows, channels, half, *refs):
    (q, k, v, g, before, after) = refs[:6]
    rim, refs = refs[-1], (None, None) + refs[:-1]
    (w_own, w_edge, w_prev, d_own, d_next, lag_in, ahead_in) = refs[8:15]
    (mid_in, q1_in, s1_in, k1_in, v1_in) = refs[15:20]
    (fsq, fsk, fsv, short, fmq, fmk, fmv, inner) = refs[20:28]
    if half:
        earlier, refs = refs[28], refs[:28] + refs[31:]
    (grad_res, grad_streams, sums_out) = refs[28:31]
    refs = refs[:27] + refs[28:]
    (sq, sk, sv, sg, sm, sw, dq, dk, dv, d1, eq, ek, ev) = refs[30:43]
    (s2_apart, w2_apart, s2_ends, w2_ends, s2_nat, w2_nat, diagonals, wins, d_wins) = refs[43:52]
    (s2_raw, w2_raw, acc, sums, moved, out_buf, sems) = refs[52:]
    now = pl.program_id(0)
    steps = pl.num_programs(0) - 1
    step = now - 1
    slot = lax.rem(now + 1, 2)
    width = TILES * LANES
    base = GROUP
    block = lane_blocks((SPAN, LANES))
    zero = jnp.zeros((), BF16)

    def copies(at_step, at_slot):
        return [
            pltpu.make_async_copy(
                out_buf.at[at_slot, x],
                grad_streams.at[
                    :,
                    pl.ds(
                        pl.multiple_of(x * channels + (half * steps + at_step) * width, width),
                        width,
                    ),
                ],
                sems.at[at_slot, x],
            )
            for x in range(3)
        ]

    def lanes_of(i):
        return pl.ds(pl.multiple_of(i * LANES, LANES), LANES)

    def slot_of(n):
        return lax.broadcasted_iota(jnp.int32, (n, LANES), 1) // GROUP % JOINED

    def pick(wide, count, lanes):
        out = wide[:count, lanes]
        for n in range(1, JOINED):
            out = jnp.where(slot_of(count) == n, wide[n * SPAN : n * SPAN + count, lanes], out)
        return out

    def window_stage(i, j):
        part = slice(j * SPAN, (j + 1) * SPAN)
        no_rows = jnp.zeros((SPAN - GROUP, LANES), BF16)
        keep = [jnp.full((SPAN, LANES), inner[n], F32).astype(BF16) for n in range(2)]
        last_w = w_edge[i]
        last_d = d_next[i, rows : rows + GROUP, :] * keep[1][:GROUP]
        if j:
            last_w = pltpu.roll(last_w, LANES - SPAN * j, 1)
            last_d = pltpu.roll(last_d, LANES - SPAN * j, 1)
        for low, high, last, out in (
            (w_prev[i, part, :] * keep[0], w_own[i, part, :], last_w, wins),
            (d_own[i, part, :], d_next[i, part, :] * keep[1], last_d, d_wins),
        ):
            win = windows(low, high, jnp.concatenate([last, no_rows], 0), block)
            for n in range(2):
                out[n, :, j * LANES : (j + 1) * LANES] = win[:, n * LANES : (n + 1) * LANES]

    def filter_stage(i, j):
        taps_part = pl.ds((i * BLOCKS + j) * JOINED * SPAN, JOINED * SPAN)
        row = lax.broadcasted_iota(jnp.int32, (JOINED * SPAN, LANES), 0) % SPAN
        lane = lax.broadcasted_iota(jnp.int32, (JOINED * SPAN, LANES), 1)
        for bands, inside, win, raw in (
            (lag_in, lane > row, wins, s2_raw),
            (ahead_in, lane >= row, d_wins, w2_raw),
        ):
            at = slice(j * LANES, (j + 1) * LANES)
            turned = bands[taps_part, :]
            over = jnp.where(inside, zero, turned)[:, :SPAN]
            raw[j % 2] = jnp.dot(
                jnp.concatenate([jnp.where(inside, turned, zero), over], 1),
                jnp.concatenate([win[0, :, at], win[1, :, at]], 1),
                preferred_element_type=F32,
            )

    def pick_stage(j):
        part = slice(j * SPAN, (j + 1) * SPAN)
        main, edge = slice(0, LANES), slice(LANES, 2 * LANES)
        for raw, apart_ref, ends_ref in ((s2_raw, s2_apart, s2_ends), (w2_raw, w2_apart, w2_ends)):
            value = raw[j % 2].astype(BF16)
            apart_ref[part, :] = pick(value, SPAN, main)
            end = pick(value, GROUP, edge)
            ends_ref[j] = pltpu.roll(end, SPAN * j, 1) if j else end

    def cross_stage(i, first):
        row = lax.broadcasted_iota(jnp.int32, (SPAN, LANES), 0)
        lane = lax.broadcasted_iota(jnp.int32, (SPAN, LANES), 1)
        nothing = jnp.zeros((SPAN, LANES), BF16)
        apart = []
        for j in (first, first + 1):
            own_d = d_own[i, j * SPAN : (j + 1) * SPAN, :]
            for n in range(JOINED):
                mine = jnp.where(slot_of(SPAN) == n, own_d, zero)
                pair = [mine, nothing] if j == first else [nothing, mine]
                apart.append(jnp.concatenate(pair, 1))
        cross = lax.dot_general(
            jnp.concatenate(apart, 0),
            wins[0, :, first * LANES : (first + 2) * LANES],
            (((1,), (1,)), ((), ())),
            preferred_element_type=F32,
        )
        for n in range(2 * JOINED):
            mine = cross[n * SPAN : (n + 1) * SPAN]
            over = jnp.concatenate(
                [mine[:, LANES:], jnp.zeros((SPAN, LANES - SPAN), F32)], 1
            )
            mine = jnp.where(lane <= row, over, mine[:, :LANES])
            diagonals[first * JOINED + n] = sum(
                pltpu.roll(mine[r : r + 8], LANES - 1 - r, 1) for r in range(0, SPAN, 8)
            )

    def natural_stage(f):
        place = lax.rem(f + 2 * TILES, 2 * TILES)
        for apart_ref, ends_ref, nat in ((s2_apart, s2_ends, s2_nat), (w2_apart, w2_ends, w2_nat)):
            parts = swap_blocks([apart_ref[j * SPAN : (j + 1) * SPAN, :] for j in range(BLOCKS)])
            for j in range(BLOCKS):
                nat[place, j * SPAN : (j + 1) * SPAN, :] = parts[j]
            end = ends_ref[0]
            for j in range(1, BLOCKS):
                end = jnp.where(lane_blocks((GROUP, LANES)) == j, ends_ref[j], end)
            nat[place, rows : rows + GROUP, :] = end

    def fold_stage(f):
        sums[pl.ds(jnp.maximum(f, 0), 1), :GROUPS, :] = fold_diagonals(
            [diagonals[j] for j in range(GROUPS)]
        )[None]

    def input_stage(i):
        lanes = lanes_of(i)
        par = lax.rem(i, 2)
        for r in range(0, rows + 2 * GROUP, GROUP):
            sm[par, r : r + GROUP, :] = mid_in[i, r : r + GROUP, :].astype(F32)
        for r in range(0, rows + GROUP, GROUP):
            sw[par, r : r + GROUP, :] = k1_in[i, r : r + GROUP, :].astype(F32) * v1_in[
                i, r : r + GROUP, :
            ].astype(F32)
        rim[0:EARLIER, :] = before[:, lanes].astype(F32) * inner[0]
        rim[LATER_AT : LATER_AT + LATER, :] = after[:, lanes].astype(F32) * inner[1]
        for x, (scratch, own) in enumerate(((sq, q), (sk, k), (sv, v))):
            at, count = EARLIER_ROWS[x]
            scratch[par, base - 2 : base, :] = rim[at + count - 2 : at + count, :]
            for r in range(0, rows, GROUP):
                scratch[par, base + r : base + r + GROUP, :] = own[r : r + GROUP, lanes].astype(F32)
        sg[0:EDGE, :] = rim[LATER_AT + 4 * EDGE : LATER_AT + LATER, :]

    def add_up(first, values, others, fresh):
        for n, other in enumerate(others):
            total = None
            for x, y in zip(values, other):
                product = x * y
                for r in range(0, GROUP, 8):
                    half = product[r : r + 8]
                    total = half if total is None else total + half
            acc[first + n] = total if fresh else acc[first + n] + total

    def element_stage(i, chunks):
        lanes = lanes_of(i)
        par = lax.rem(i, 2)
        place = lax.rem(step * TILES + i + 2 * TILES, 2 * TILES)
        main = chunks[0] < GROUPS
        fresh = chunks[0] == GROUPS - 1
        mq, mk, mv = taps_of(fmq, lanes), taps_of(fmk, lanes), taps_of(fmv, lanes)
        starts = [a * GROUP for a in chunks]
        at = lambda ref, t: ref[t : t + GROUP, :]
        gs = [g[t : t + GROUP, lanes].astype(F32) if main else sg[...] for t in starts]
        tall = lambda ref, t: ref[par, t : t + GROUP, :]
        mids = [[tall(sm, base + t - n) for t in starts] for n in range(3)]
        parts = [[], [], []]
        for c, t in enumerate(starts):
            m = [mids[n][c] for n in range(3)]
            k2 = mk[0] * m[0] + mk[1] * m[1] + mk[2] * m[2]
            v2 = mv[0] * m[0] + mv[1] * m[1] + mv[2] * m[2]
            s2 = s2_nat[place, t : t + GROUP, :].astype(F32)
            w2 = w2_nat[place, t : t + GROUP, :].astype(F32)
            for x, (ref, value) in enumerate(
                zip((dq, dk, dv), (gs[c] * s2, w2 * v2, w2 * k2))
            ):
                ref[t : t + GROUP, :] = value
                parts[x].append(value)
        if main:
            for x in range(3):
                add_up(9 + 3 * x, parts[x], mids, fresh)
        slopes = []
        for c, t in enumerate(starts):
            dmid = (
                gs[c]
                + ahead_taps(mq, dq, t, GROUP)
                + ahead_taps(mk, dk, t, GROUP)
                + ahead_taps(mv, dv, t, GROUP)
            )
            if main:
                grad_res[t : t + GROUP, lanes] = dmid.astype(BF16)
            slope = dmid * q1_in[i, t : t + GROUP, :].astype(F32)
            d1[t : t + GROUP, :] = slope
            slopes.append(slope)
            eq[t : t + GROUP, :] = dmid * s1_in[i, t : t + GROUP, :].astype(F32)
        ts = taps_of(short, lanes)
        if main:
            lagged = [[tall(sw, base + t - n) for t in starts] for n in range(len(ts))]
            add_up(18, slopes, lagged, fresh)
        for t in starts:
            dw1 = ahead_taps(ts, d1, t, GROUP)
            ek[t : t + GROUP, :] = dw1 * v1_in[i, base + t : base + t + GROUP, :].astype(F32)
            ev[t : t + GROUP, :] = dw1 * k1_in[i, base + t : base + t + GROUP, :].astype(F32)
        if not main:
            return
        for x, (ref, taps_ref, stream) in enumerate(((eq, fsq, sq), (ek, fsk, sk), (ev, fsv, sv))):
            taps = taps_of(taps_ref, lanes)
            for t in starts:
                out_buf[slot, x, t : t + GROUP, lanes] = ahead_taps(taps, ref, t, GROUP).astype(
                    BF16
                )
            add_up(
                3 * x,
                [at(ref, t) for t in starts],
                [[tall(stream, base + t - n) for t in starts] for n in range(3)],
                fresh,
            )

    def totals_stage(i):
        tile = pl.ds(jnp.maximum(step * TILES + i, 0), 1)
        for n in range(0, 24, 8):
            sums[tile, GROUPS + n : GROUPS + n + 8, :] = fold_rows(
                [acc[n + j] for j in range(8)]
            )[None]
        sums[tile, 32:33, :] = jnp.sum(acc[24], axis=0, keepdims=True)[None]

    @pl.when(now == 0)
    def _():
        for ref in (sg, dq, dk, dv, d1, eq, ek, ev):
            ref[...] = jnp.zeros(ref.shape, F32)

    @pl.when(step >= 2)
    def _():
        for copy in copies(step - 2, slot):
            copy.wait()

    def send_out():
        tiles = sums.shape[0]
        of = lambda tile: earlier if half and tile < tiles else sums
        for to in range(moved.shape[0]):
            for place in range(3):
                x, tile = divmod(3 * to + place, moved.shape[0])
                for n in range(3):
                    for row in (GROUPS, GROUPS + 9):
                        at, source = row + 3 * n + place, row + 3 * x + n
                        moved[to, at : at + 1, :] = of(tile)[
                            tile % tiles, source : source + 1, :
                        ]
            moved[to, :GROUPS, :] = of(to)[to % tiles, :GROUPS, :]
            moved[to, 26:33, :] = of(to)[to % tiles, 26:33, :]
        sums_out[...] = moved[:, :33, :].astype(BF16)

    def one_tile(filtering, differentiating):
        def run(i, carry):
            flat = now * TILES + i
            for j in reversed(range(BLOCKS)):

                @pl.when(i >= 0)
                def _():
                    if filtering:
                        if j == 3:
                            fold_stage(flat - 1)
                            pick_stage(0)
                        else:
                            if j == 2:
                                natural_stage(flat - 1)
                            pick_stage(j + 1)
                        filter_stage(i, j)
                        if j == 2:
                            cross_stage(i, 2)
                        if j == 0:
                            cross_stage(i, 0)
                        if j:
                            window_stage(i, j - 1)
                        else:
                            window_stage(jnp.minimum(i + 1, TILES - 1), BLOCKS - 1)
                    if differentiating:
                        element_stage(i, list(reversed(range(j * JOINED, (j + 1) * JOINED))))
                        if j == 1:
                            following = jnp.minimum(i + 1, TILES - 1)
                            input_stage(following)
                            element_stage(following, [GROUPS])
                        if j == 0:
                            totals_stage(i)

            return carry

        return run

    @pl.when(now == 0)
    def _():
        window_stage(0, BLOCKS - 1)
        lax.fori_loop(0, TILES, one_tile(True, False), 0)

    @pl.when(jnp.logical_and(now > 0, now < steps))
    def _():
        window_stage(0, BLOCKS - 1)
        input_stage(0)
        element_stage(0, [GROUPS])
        lax.fori_loop(0, TILES, one_tile(True, True), 0)

    @pl.when(now == steps)
    def _():
        fold_stage(now * TILES - 1)
        pick_stage(0)
        natural_stage(now * TILES - 1)
        input_stage(0)
        element_stage(0, [GROUPS])
        lax.fori_loop(0, TILES, one_tile(False, True), 0)

    @pl.when(step >= 0)
    def _():
        for copy in copies(step, slot):
            copy.start()

    @pl.when(now == steps)
    def _():
        if half == HALVES - 1:
            send_out()
        else:
            sums_out[...] = sums[...]

        @pl.when(steps > 1)
        def _():
            for copy in copies(step - 1, 1 - slot):
                copy.wait()

        for copy in copies(step, slot):
            copy.wait()


def last_kernel(scale, first, second, third, fourth, fs_out, fm_out, short_out, medium_out):
    total = (first[...] + second[...] + third[...] + fourth[...]) * scale
    for out, row in ((fs_out, 8), (fm_out, 17)):
        for n in range(9):
            lanes = slice(n % 3 * LANES, (n % 3 + 1) * LANES)
            out[n // 3 : n // 3 + 1, lanes] = total[row + n : row + n + 1]
    short_out[...] = total[26:33]
    row = lax.broadcasted_iota(jnp.int32, (LANES, LANES), 0)
    lane = lax.broadcasted_iota(jnp.int32, (LANES, LANES), 1)
    flip = jnp.where(row + lane == LANES - 1, 1.0, 0.0).astype(F32)
    medium_out[...] = lax.dot_general(
        total[0:8],
        flip,
        (((1,), (1,)), ((), ())),
        precision=lax.Precision.HIGHEST,
        preferred_element_type=F32,
    )


def columns(rows, first=0):
    width = TILES * LANES
    return pl.BlockSpec((rows, width), lambda j: (0, first + j))


def moved_spec(spec, move):
    return pl.BlockSpec(spec.block_shape, lambda j: spec.index_map(move(j)))


def tiled(rows):
    return pl.BlockSpec((TILES, rows, LANES), lambda j: (j, 0, 0))


def shards(
    residual_in, se_streams, cotangent, feat_short, feat_medium, short_filter, medium_filter_weight
):
    res, streams, g = residual_in[0], se_streams[0], cotangent[0]
    rows, channels = res.shape
    seqs, slabs = lax.axis_size("seq"), lax.axis_size("dp")
    tiles = channels // LANES
    steps = tiles // TILES
    groups = medium_filter_weight.shape[1]
    cut = channels // 2
    strip = lambda x, down: pl.BlockSpec((GROUP, cut), lambda j: (down, 2 * x + j))
    last = rows // GROUP - 1
    before, after = pl.pallas_call(
        rim_kernel,
        grid=(2,),
        in_specs=[strip(x, last) for x in (0, 1, 2, 0)] + [strip(x, 0) for x in (0, 1, 2, 0, 0)],
        out_specs=[pl.BlockSpec((n, cut), lambda j: (0, j)) for n in (EARLIER, LATER)],
        out_shape=[jax.ShapeDtypeStruct((n, channels), BF16) for n in (EARLIER, LATER)],
        scratch_shapes=[pltpu.VMEM((LATER_AT + LATER + 6, LANES), F32)],
        compiler_params=pltpu.CompilerParams(vmem_limit_bytes=63 * 1024 * 1024),
        name="rims",
    )(*[streams] * 3, res, *[streams] * 3, res, g)
    before, after = turn(before, "seq", 1), turn(after, "seq", -1)
    seq = lax.axis_index("seq")
    inner = jnp.stack([seq > 0, seq < seqs - 1]).astype(F32)
    bands = pl.BlockSpec((LANES * SPAN, LANES), lambda j: (j, 0))
    lag, ahead = pl.pallas_call(
        toeplitz_kernel,
        grid=(groups // LANES,),
        in_specs=[pl.BlockSpec((LANES, LANES), lambda j: (0, j))],
        out_specs=[bands] * 2,
        out_shape=[jax.ShapeDtypeStruct((groups * SPAN, LANES), BF16)] * 2,
        scratch_shapes=[pltpu.VMEM((LANES, LANES), F32)] * 2,
        name="toeplitz",
    )(medium_filter_weight)
    inner, lag, ahead = lax.optimization_barrier((inner, lag, ahead))
    half_tiles = tiles // HALVES
    half_steps = half_tiles // TILES
    filters = (feat_short,) * 3 + (short_filter,) + (feat_medium,) * 3
    long, ext = rows + 2 * GROUP, rows + GROUP
    saved = [long, ext, ext, long, long]
    in_smem = pl.BlockSpec(memory_space=pltpu.SMEM)
    anywhere = pl.BlockSpec(memory_space=pl.ANY)
    limit = pltpu.CompilerParams(vmem_limit_bytes=63 * 1024 * 1024)
    scratch = pltpu.VMEM((FRAME + ext, LANES), F32)
    row_buf = lambda n: pltpu.VMEM((n, LANES), F32)
    behind = lambda spec: moved_spec(spec, lambda j: jnp.maximum(j - 1, 0))
    ahead_of = lambda spec: moved_spec(spec, lambda j: jnp.minimum(j, half_steps - 1))

    def specs_of(half):
        block = lambda n: lambda x: columns(n, x * steps + half * half_steps)
        filter_specs = (
            [block(3)(x) for x in range(3)]
            + [block(short_filter.shape[0])(0)]
            + [block(3)(x) for x in range(3)]
        )
        return block(rows), [block(EARLIER)(0), block(LATER)(0)], filter_specs

    def products(half):
        whole, edge, filter_specs = specs_of(half)
        return pl.pallas_call(
            functools.partial(first_kernel, rows),
            grid=(half_steps,),
            in_specs=[whole(x) for x in range(3)]
            + [whole(0)] * 2
            + edge
            + filter_specs
            + [in_smem],
            out_specs=[tiled(rows), tiled(GROUP), tiled(ext)] + [tiled(n) for n in saved],
            out_shape=[
                jax.ShapeDtypeStruct((half_tiles, n, LANES), BF16)
                for n in [rows, GROUP, ext] + saved
            ],
            scratch_shapes=[scratch] * 7 + [row_buf(LATER_AT + LATER + 6)],
            compiler_params=limit,
            name="products",
        )(*[streams] * 3, res, g, before, after, *filters, inner)

    def gradients(half, made, w_prev, d_next, earlier):
        whole, edge, filter_specs = specs_of(half)
        w_own, w_edge, d_own, *kept = made
        per_step = pl.BlockSpec(
            (TILES * GROUPS * SPAN, LANES), lambda j: (half * half_steps + j, 0)
        )
        raw_sums = jax.ShapeDtypeStruct((half_tiles, 40, LANES), F32)
        all_sums = jax.ShapeDtypeStruct((tiles, 33, LANES), BF16)
        own_sums = pl.BlockSpec((half_tiles, 40, LANES), lambda j: (0, 0, 0))
        own_shares = pl.BlockSpec((tiles, 33, LANES), lambda j: (0, 0, 0))
        last = half == HALVES - 1
        first_in = [whole(x) for x in range(3)] + [whole(0)] + edge
        return pl.pallas_call(
            functools.partial(second_kernel, rows, channels, half),
            grid=(half_steps + 1,),
            in_specs=[behind(spec) for spec in first_in]
            + [
                ahead_of(spec)
                for spec in [tiled(rows), tiled(GROUP), tiled(rows), tiled(ext), tiled(ext)]
                + [per_step] * 2
            ]
            + [behind(spec) for spec in [tiled(n) for n in saved] + filter_specs]
            + [in_smem]
            + ([own_sums, anywhere, anywhere] if half else []),
            out_specs=[behind(whole(0)), anywhere] + [own_shares if last else own_sums],
            out_shape=[
                jax.ShapeDtypeStruct((rows, channels), BF16),
                jax.ShapeDtypeStruct((rows, 3 * channels), BF16),
            ]
            + [all_sums if last else raw_sums],
            input_output_aliases={27: 0, 28: 1} if half else {},
            scratch_shapes=[pltpu.VMEM((2, GROUP + rows, LANES), F32)] * 3
            + [row_buf(GROUP)]
            + [pltpu.VMEM((2, n, LANES), F32) for n in (long, ext)]
            + [row_buf(ext + 8)] * 7
            + [pltpu.VMEM((rows, LANES), BF16)] * 2
            + [pltpu.VMEM((BLOCKS, GROUP, LANES), BF16)] * 2
            + [pltpu.VMEM((2 * TILES, ext, LANES), BF16)] * 2
            + [pltpu.VMEM((GROUPS, 8, LANES), F32)]
            + [pltpu.VMEM((2, LANES + SPAN, BLOCKS * LANES), BF16)] * 2
            + [pltpu.VMEM((2, JOINED * SPAN, 2 * LANES), F32)] * 2
            + [
                pltpu.VMEM((25, 8, LANES), F32),
                pltpu.VMEM((half_tiles, 40, LANES), F32),
                pltpu.VMEM((tiles, 40, LANES), F32),
                pltpu.VMEM((2, 3, rows, TILES * LANES), BF16),
                pltpu.SemaphoreType.DMA((2, 3)),
                row_buf(LATER_AT + LATER + 6),
            ],
            compiler_params=limit,
            name="gradients",
        )(
            *[streams] * 3, g, before, after,
            w_own, w_edge, w_prev, d_own, d_next, lag, ahead,
            *kept, *filters, inner, *earlier
        )

    made, arrived = [], []
    for half in range(HALVES):
        made.append(products(half))
        arrived.append((turn(made[half][0], "seq", 1), turn(made[half][2], "seq", -1)))
    earlier = ()
    for half in range(HALVES):
        grad_res, grad_streams, sums = gradients(half, made[half], *arrived[half], earlier)
        earlier = (sums, grad_res, grad_streams)
    norm_factor = 1.0 / math.sqrt(slabs * seqs * rows)
    parts = lax.all_to_all(sums, "seq", split_axis=0, concat_axis=0, tiled=True)
    share = jnp.sum(parts.astype(F32), axis=0)
    others = [turn(share, "dp", n) for n in range(1, slabs)]
    cols = 3 * channels // tiles
    filter_grads = pl.pallas_call(
        functools.partial(last_kernel, norm_factor),
        out_shape=[
            jax.ShapeDtypeStruct(shape, F32)
            for shape in ((3, cols), (3, cols), (7, LANES), (GROUPS, LANES))
        ],
        name="totals",
    )(share, *others)
    return (grad_res[None], grad_streams[None], *filter_grads[:3], filter_grads[3].T)


def solution(mesh):
    placed = (P("dp", "seq", None), P("dp", "seq", None), P("dp", "seq", None), P(), P(), P(), P())
    return jax.shard_map(
        shards,
        mesh=mesh,
        in_specs=placed,
        out_specs=(
            P("dp", "seq", None),
            P("dp", "seq", None),
            P(None, "seq"),
            P(None, "seq"),
            P(None, "seq"),
            P(None, "seq"),
        ),
        check_vma=False,
    )
```

```python
import functools
import math

import jax
import jax.numpy as jnp
from jax import lax
from jax.experimental import pallas as pl
from jax.experimental.pallas import tpu as pltpu
from jax.sharding import PartitionSpec as P

F32 = jnp.float32
BF16 = jnp.bfloat16
LANES = 128
GROUP = 16
GROUPS = LANES // GROUP
SPAN = 32
BLOCKS = LANES // SPAN
JOINED = SPAN // GROUP
EDGE = 10
EARLIER_ROWS = ((20, 4), (0, 10), (10, 10), (24, 2))
EARLIER = 26
LATER = 5 * EDGE
LATER_AT = 32
FRAME = 24
HALVES = 1
VMEM = 65408 * 1024
TILES = 4


def turn(array, axis, by):
    peers = lax.axis_size(axis)
    return lax.ppermute(array, axis, [(i, (i + by) % peers) for i in range(peers)])


def lane_blocks(shape):
    return lax.broadcasted_iota(jnp.int32, shape, 1) // SPAN


def swap_blocks(parts):
    parts = list(parts)
    block = lane_blocks(parts[0].shape)
    step = BLOCKS // 2
    while step:
        low = (block & step) == 0
        shift = SPAN * step
        for i in range(BLOCKS):
            if i & step == 0:
                first, second = parts[i], parts[i + step]
                parts[i] = jnp.where(low, first, pltpu.roll(second, shift, 1))
                parts[i + step] = jnp.where(low, pltpu.roll(first, LANES - shift, 1), second)
        step //= 2
    return parts


def taps_of(ref, lanes):
    return [ref[i : i + 1, lanes] for i in range(ref.shape[0])]


def back_taps(taps, ref, start, rows):
    total = taps[0] * ref[start : start + rows, :]
    for i in range(1, len(taps)):
        total = total + taps[i] * ref[start - i : start - i + rows, :]
    return total


def ahead_taps(taps, ref, start, rows):
    total = taps[0] * ref[start : start + rows, :]
    for i in range(1, len(taps)):
        total = total + taps[i] * ref[start + i : start + i + rows, :]
    return total


def rim_kernel(lq, lk, lv, lr, fq, fk, fv, fr, fg, before, after, rim):
    for c in range(0, before.shape[1], LANES):
        lanes = slice(c, c + LANES)
        for at, ref in ((16, lr), (14, lq), (10, lv), (0, lk)):
            rim[at : at + GROUP, :] = ref[:, lanes].astype(F32)
        before[:, lanes] = rim[GROUP - EDGE : GROUP - EDGE + EARLIER, :].astype(BF16)
        for x, ref in enumerate((fq, fk, fv, fr, fg)):
            at = LATER_AT + EDGE * x
            rim[at : at + GROUP, :] = ref[:, lanes].astype(F32)
        after[:, lanes] = rim[LATER_AT : LATER_AT + LATER, :].astype(BF16)


def first_kernel(rows, *refs):
    (q, k, v, res, g, before, after) = refs[:7]
    (fsq, fsk, fsv, short, fmq, fmk, fmv, inner) = refs[7:15]
    (w_own, w_edge, d_own, mid_out, q1_out, s1_out, k1_out, v1_out) = refs[15:23]
    (sq, sk, sv, sr, sg, sw, sm, rim) = refs[23:]
    total = rows + GROUP

    @pl.when(pl.program_id(0) == 0)
    def _():
        for ref in (sq, sk, sv, sr, sg):
            ref[...] = jnp.zeros(ref.shape, F32)

    def one_tile(i, carry):
        lanes = pl.ds(pl.multiple_of(i * LANES, LANES), LANES)
        rim[0:EARLIER, :] = before[:, lanes].astype(F32) * inner[0]
        rim[LATER_AT : LATER_AT + LATER, :] = after[:, lanes].astype(F32) * inner[1]
        for x, (scratch, own) in enumerate(((sq, q), (sk, k), (sv, v), (sr, res), (sg, g))):
            if x < 4:
                at, count = EARLIER_ROWS[x]
                scratch[FRAME - count : FRAME, :] = rim[at : at + count, :]
            for r in range(0, rows, GROUP):
                scratch[FRAME + r : FRAME + r + GROUP, :] = own[r : r + GROUP, lanes].astype(F32)
            at = LATER_AT + EDGE * x
            scratch[FRAME + rows : FRAME + rows + EDGE, :] = rim[at : at + EDGE, :]
        tq, tk, tv = taps_of(fsq, lanes), taps_of(fsk, lanes), taps_of(fsv, lanes)
        for t in range(-GROUP, total, GROUP):
            at = FRAME + t
            k1 = back_taps(tk, sk, at, GROUP)
            v1 = back_taps(tv, sv, at, GROUP)
            sw[at : at + GROUP, :] = k1 * v1
            k1_out[i, t + GROUP : t + 2 * GROUP, :] = k1.astype(BF16)
            v1_out[i, t + GROUP : t + 2 * GROUP, :] = v1.astype(BF16)
        ts = taps_of(short, lanes)
        for t in range(-GROUP, total, GROUP):
            at = FRAME + t
            q1 = back_taps(tq, sq, at, GROUP)
            s1 = back_taps(ts, sw, at, GROUP)
            mid = (sr[at : at + GROUP, :] + q1 * s1).astype(BF16)
            sm[at : at + GROUP, :] = mid.astype(F32)
            mid_out[i, t + GROUP : t + 2 * GROUP, :] = mid
            if t >= 0:
                q1_out[i, t : t + GROUP, :] = q1.astype(BF16)
                s1_out[i, t : t + GROUP, :] = s1.astype(BF16)
        mq, mk, mv = taps_of(fmq, lanes), taps_of(fmk, lanes), taps_of(fmv, lanes)
        products, slopes = [], []
        for t in range(0, total, GROUP):
            at = FRAME + t
            m = [sm[at - j : at - j + GROUP, :] for j in range(3)]
            q2, k2, v2 = [
                taps[0] * m[0] + taps[1] * m[1] + taps[2] * m[2] for taps in (mq, mk, mv)
            ]
            products.append((k2 * v2).astype(BF16))
            slopes.append((sg[at : at + GROUP, :] * q2).astype(BF16))
        for values, own in ((products, w_own), (slopes, d_own)):
            parts = [
                jnp.concatenate(values[j : j + JOINED], 0)
                for j in range(0, GROUPS, JOINED)
            ]
            for j, part in enumerate(swap_blocks(parts)):
                own[i, j * SPAN : (j + 1) * SPAN, :] = part
        w_edge[i] = products[GROUPS]
        d_own[i, rows : rows + GROUP, :] = slopes[GROUPS]
        return carry

    lax.fori_loop(0, TILES, one_tile, 0)


def windows(low, high, last, block):
    rows = []
    for k in range(BLOCKS + 1):
        if k == 0:
            first, second = low, high
        elif k == BLOCKS:
            first, second = high, last
        else:
            shift = LANES - SPAN * k
            second = pltpu.roll(high, shift, 1)
            first = jnp.where(block < BLOCKS - k, pltpu.roll(low, shift, 1), second)
        rows.append(jnp.concatenate([first, second], 1))
    return jnp.concatenate(rows, 0)


def fold_diagonals(parts):
    row = lax.broadcasted_iota(jnp.int32, parts[0].shape, 0)
    half = len(parts) // 2
    while half:
        first = (row & half) == 0
        folded = []
        for x, y in zip(parts[:half], parts[half:]):
            low = jnp.where(first, x, pltpu.roll(y, half, 0))
            high = jnp.where(first, pltpu.roll(x, 8 - half, 0), y)
            folded.append(low + pltpu.roll(high, LANES - half, 1))
        parts = folded
        half //= 2
    return parts[0]


def fold_rows(parts):
    row = lax.broadcasted_iota(jnp.int32, parts[0].shape, 0)
    half = len(parts) // 2
    while half:
        first = (row & half) == 0
        parts = [
            jnp.where(first, x, pltpu.roll(y, half, 0))
            + jnp.where(first, pltpu.roll(x, 8 - half, 0), y)
            for x, y in zip(parts[:half], parts[half:])
        ]
        half //= 2
    return parts[0]


def toeplitz_kernel(taps, lag_out, ahead_out, taps_fwd, taps_rev):
    row = lax.broadcasted_iota(jnp.int32, (LANES, LANES), 0)
    lane = lax.broadcasted_iota(jnp.int32, (LANES, LANES), 1)
    for out, places in ((taps_fwd, row == lane), (taps_rev, row + lane == LANES - 1)):
        out[...] = lax.dot_general(
            taps[...],
            jnp.where(places, 1.0, 0.0).astype(BF16),
            (((0,), (0,)), ((), ())),
            preferred_element_type=F32,
        )
    shape = (SPAN, LANES)
    for j in range(LANES):
        part = slice(j * SPAN, (j + 1) * SPAN)
        for taps, first, out in ((taps_fwd, 0, ahead_out), (taps_rev, 1, lag_out)):
            turned = pltpu.roll(
                jnp.broadcast_to(taps[j : j + 1, :], shape), first, 1, stride=1, stride_axis=0
            )
            out[part, :] = turned.astype(BF16)


def second_kernel(rows, channels, half, *refs):
    (q, k, v, g, before, after) = refs[:6]
    rim, refs = refs[-1], (None, None) + refs[:-1]
    (w_own, w_edge, w_prev, d_own, d_next, lag_in, ahead_in) = refs[8:15]
    (mid_in, q1_in, s1_in, k1_in, v1_in) = refs[15:20]
    (fsq, fsk, fsv, short, fmq, fmk, fmv, inner) = refs[20:28]
    if half:
        earlier, refs = refs[28], refs[:28] + refs[31:]
    (grad_res, grad_streams, sums_out) = refs[28:31]
    refs = refs[:27] + refs[28:]
    (sq, sk, sv, sg, sm, sw, dq, dk, dv, d1, eq, ek, ev) = refs[30:43]
    (s2_apart, w2_apart, s2_ends, w2_ends, s2_nat, w2_nat, diagonals, wins, d_wins) = refs[43:52]
    (s2_raw, w2_raw, acc, sums, moved, out_buf, sems) = refs[52:]
    now = pl.program_id(0)
    steps = pl.num_programs(0) - 1
    step = now - 1
    slot = lax.rem(now + 1, 2)
    width = TILES * LANES
    base = GROUP
    block = lane_blocks((SPAN, LANES))
    zero = jnp.zeros((), BF16)

    def copies(at_step, at_slot):
        return [
            pltpu.make_async_copy(
                out_buf.at[at_slot, x],
                grad_streams.at[
                    :,
                    pl.ds(
                        pl.multiple_of(x * channels + (half * steps + at_step) * width, width),
                        width,
                    ),
                ],
                sems.at[at_slot, x],
            )
            for x in range(3)
        ]

    def lanes_of(i):
        return pl.ds(pl.multiple_of(i * LANES, LANES), LANES)

    def slot_of(n):
        return lax.broadcasted_iota(jnp.int32, (n, LANES), 1) // GROUP % JOINED

    def pick(wide, count, lanes):
        out = wide[:count, lanes]
        for n in range(1, JOINED):
            out = jnp.where(slot_of(count) == n, wide[n * SPAN : n * SPAN + count, lanes], out)
        return out

    def window_stage(i, j):
        part = slice(j * SPAN, (j + 1) * SPAN)
        no_rows = jnp.zeros((SPAN - GROUP, LANES), BF16)
        keep = [jnp.full((SPAN, LANES), inner[n], F32).astype(BF16) for n in range(2)]
        last_w = w_edge[i]
        last_d = d_next[i, rows : rows + GROUP, :] * keep[1][:GROUP]
        if j:
            last_w = pltpu.roll(last_w, LANES - SPAN * j, 1)
            last_d = pltpu.roll(last_d, LANES - SPAN * j, 1)
        for low, high, last, out in (
            (w_prev[i, part, :] * keep[0], w_own[i, part, :], last_w, wins),
            (d_own[i, part, :], d_next[i, part, :] * keep[1], last_d, d_wins),
        ):
            win = windows(low, high, jnp.concatenate([last, no_rows], 0), block)
            for n in range(2):
                out[n, :, j * LANES : (j + 1) * LANES] = win[:, n * LANES : (n + 1) * LANES]

    def filter_stage(i, j):
        taps_part = pl.ds((i * BLOCKS + j) * JOINED * SPAN, JOINED * SPAN)
        row = lax.broadcasted_iota(jnp.int32, (JOINED * SPAN, LANES), 0) % SPAN
        lane = lax.broadcasted_iota(jnp.int32, (JOINED * SPAN, LANES), 1)
        for bands, inside, win, raw in (
            (lag_in, lane > row, wins, s2_raw),
            (ahead_in, lane >= row, d_wins, w2_raw),
        ):
            at = slice(j * LANES, (j + 1) * LANES)
            turned = bands[taps_part, :]
            over = jnp.where(inside, zero, turned)[:, :SPAN]
            raw[j % 2] = jnp.dot(
                jnp.concatenate([jnp.where(inside, turned, zero), over], 1),
                jnp.concatenate([win[0, :, at], win[1, :, at]], 1),
                preferred_element_type=F32,
            )

    def pick_stage(j):
        part = slice(j * SPAN, (j + 1) * SPAN)
        main, edge = slice(0, LANES), slice(LANES, 2 * LANES)
        for raw, apart_ref, ends_ref in ((s2_raw, s2_apart, s2_ends), (w2_raw, w2_apart, w2_ends)):
            value = raw[j % 2].astype(BF16)
            apart_ref[part, :] = pick(value, SPAN, main)
            end = pick(value, GROUP, edge)
            ends_ref[j] = pltpu.roll(end, SPAN * j, 1) if j else end

    def cross_stage(i, first):
        row = lax.broadcasted_iota(jnp.int32, (SPAN, LANES), 0)
        lane = lax.broadcasted_iota(jnp.int32, (SPAN, LANES), 1)
        nothing = jnp.zeros((SPAN, LANES), BF16)
        apart = []
        for j in (first, first + 1):
            own_d = d_own[i, j * SPAN : (j + 1) * SPAN, :]
            for n in range(JOINED):
                mine = jnp.where(slot_of(SPAN) == n, own_d, zero)
                pair = [mine, nothing] if j == first else [nothing, mine]
                apart.append(jnp.concatenate(pair, 1))
        cross = lax.dot_general(
            jnp.concatenate(apart, 0),
            wins[0, :, first * LANES : (first + 2) * LANES],
            (((1,), (1,)), ((), ())),
            preferred_element_type=F32,
        )
        for n in range(2 * JOINED):
            mine = cross[n * SPAN : (n + 1) * SPAN]
            over = jnp.concatenate(
                [mine[:, LANES:], jnp.zeros((SPAN, LANES - SPAN), F32)], 1
            )
            mine = jnp.where(lane <= row, over, mine[:, :LANES])
            diagonals[first * JOINED + n] = sum(
                pltpu.roll(mine[r : r + 8], LANES - 1 - r, 1) for r in range(0, SPAN, 8)
            )

    def natural_stage(f):
        place = lax.rem(f + 2 * TILES, 2 * TILES)
        for apart_ref, ends_ref, nat in ((s2_apart, s2_ends, s2_nat), (w2_apart, w2_ends, w2_nat)):
            parts = swap_blocks([apart_ref[j * SPAN : (j + 1) * SPAN, :] for j in range(BLOCKS)])
            for j in range(BLOCKS):
                nat[place, j * SPAN : (j + 1) * SPAN, :] = parts[j]
            end = ends_ref[0]
            for j in range(1, BLOCKS):
                end = jnp.where(lane_blocks((GROUP, LANES)) == j, ends_ref[j], end)
            nat[place, rows : rows + GROUP, :] = end

    def fold_stage(f):
        sums[pl.ds(jnp.maximum(f, 0), 1), :GROUPS, :] = fold_diagonals(
            [diagonals[j] for j in range(GROUPS)]
        )[None]

    def input_stage(i):
        lanes = lanes_of(i)
        par = lax.rem(i, 2)
        for r in range(0, rows + 2 * GROUP, GROUP):
            sm[par, r : r + GROUP, :] = mid_in[i, r : r + GROUP, :].astype(F32)
        for r in range(0, rows + GROUP, GROUP):
            sw[par, r : r + GROUP, :] = k1_in[i, r : r + GROUP, :].astype(F32) * v1_in[
                i, r : r + GROUP, :
            ].astype(F32)
        rim[0:EARLIER, :] = before[:, lanes].astype(F32) * inner[0]
        rim[LATER_AT : LATER_AT + LATER, :] = after[:, lanes].astype(F32) * inner[1]
        for x, (scratch, own) in enumerate(((sq, q), (sk, k), (sv, v))):
            at, count = EARLIER_ROWS[x]
            scratch[par, base - 2 : base, :] = rim[at + count - 2 : at + count, :]
            for r in range(0, rows, GROUP):
                scratch[par, base + r : base + r + GROUP, :] = own[r : r + GROUP, lanes].astype(F32)
        sg[0:EDGE, :] = rim[LATER_AT + 4 * EDGE : LATER_AT + LATER, :]

    def add_up(first, values, others, fresh):
        for n, other in enumerate(others):
            total = None
            for x, y in zip(values, other):
                product = x * y
                for r in range(0, GROUP, 8):
                    half = product[r : r + 8]
                    total = half if total is None else total + half
            acc[first + n] = total if fresh else acc[first + n] + total

    def element_stage(i, chunks):
        lanes = lanes_of(i)
        par = lax.rem(i, 2)
        place = lax.rem(step * TILES + i + 2 * TILES, 2 * TILES)
        main = chunks[0] < GROUPS
        fresh = chunks[0] == GROUPS - 1
        mq, mk, mv = taps_of(fmq, lanes), taps_of(fmk, lanes), taps_of(fmv, lanes)
        starts = [a * GROUP for a in chunks]
        at = lambda ref, t: ref[t : t + GROUP, :]
        gs = [g[t : t + GROUP, lanes].astype(F32) if main else sg[...] for t in starts]
        tall = lambda ref, t: ref[par, t : t + GROUP, :]
        mids = [[tall(sm, base + t - n) for t in starts] for n in range(3)]
        parts = [[], [], []]
        for c, t in enumerate(starts):
            m = [mids[n][c] for n in range(3)]
            k2 = mk[0] * m[0] + mk[1] * m[1] + mk[2] * m[2]
            v2 = mv[0] * m[0] + mv[1] * m[1] + mv[2] * m[2]
            s2 = s2_nat[place, t : t + GROUP, :].astype(F32)
            w2 = w2_nat[place, t : t + GROUP, :].astype(F32)
            for x, (ref, value) in enumerate(
                zip((dq, dk, dv), (gs[c] * s2, w2 * v2, w2 * k2))
            ):
                ref[t : t + GROUP, :] = value
                parts[x].append(value)
        if main:
            for x in range(3):
                add_up(9 + 3 * x, parts[x], mids, fresh)
        slopes = []
        for c, t in enumerate(starts):
            dmid = (
                gs[c]
                + ahead_taps(mq, dq, t, GROUP)
                + ahead_taps(mk, dk, t, GROUP)
                + ahead_taps(mv, dv, t, GROUP)
            )
            if main:
                grad_res[t : t + GROUP, lanes] = dmid.astype(BF16)
            slope = dmid * q1_in[i, t : t + GROUP, :].astype(F32)
            d1[t : t + GROUP, :] = slope
            slopes.append(slope)
            eq[t : t + GROUP, :] = dmid * s1_in[i, t : t + GROUP, :].astype(F32)
        ts = taps_of(short, lanes)
        if main:
            lagged = [[tall(sw, base + t - n) for t in starts] for n in range(len(ts))]
            add_up(18, slopes, lagged, fresh)
        for t in starts:
            dw1 = ahead_taps(ts, d1, t, GROUP)
            ek[t : t + GROUP, :] = dw1 * v1_in[i, base + t : base + t + GROUP, :].astype(F32)
            ev[t : t + GROUP, :] = dw1 * k1_in[i, base + t : base + t + GROUP, :].astype(F32)
        if not main:
            return
        for x, (ref, taps_ref, stream) in enumerate(((eq, fsq, sq), (ek, fsk, sk), (ev, fsv, sv))):
            taps = taps_of(taps_ref, lanes)
            for t in starts:
                out_buf[slot, x, t : t + GROUP, lanes] = ahead_taps(taps, ref, t, GROUP).astype(
                    BF16
                )
            add_up(
                3 * x,
                [at(ref, t) for t in starts],
                [[tall(stream, base + t - n) for t in starts] for n in range(3)],
                fresh,
            )

    def totals_stage(i):
        tile = pl.ds(jnp.maximum(step * TILES + i, 0), 1)
        for n in range(0, 24, 8):
            sums[tile, GROUPS + n : GROUPS + n + 8, :] = fold_rows(
                [acc[n + j] for j in range(8)]
            )[None]
        sums[tile, 32:33, :] = jnp.sum(acc[24], axis=0, keepdims=True)[None]

    @pl.when(now == 0)
    def _():
        for ref in (sg, dq, dk, dv, d1, eq, ek, ev):
            ref[...] = jnp.zeros(ref.shape, F32)

    @pl.when(step >= 2)
    def _():
        for copy in copies(step - 2, slot):
            copy.wait()

    def send_out():
        tiles = sums.shape[0]
        of = lambda tile: earlier if half and tile < tiles else sums
        for to in range(moved.shape[0]):
            for place in range(3):
                x, tile = divmod(3 * to + place, moved.shape[0])
                for n in range(3):
                    for row in (GROUPS, GROUPS + 9):
                        at, source = row + 3 * n + place, row + 3 * x + n
                        moved[to, at : at + 1, :] = of(tile)[
                            tile % tiles, source : source + 1, :
                        ]
            moved[to, :GROUPS, :] = of(to)[to % tiles, :GROUPS, :]
            moved[to, 26:33, :] = of(to)[to % tiles, 26:33, :]
        sums_out[...] = moved[:, :33, :].astype(BF16)

    def one_tile(filtering, differentiating):
        def run(i, carry):
            flat = now * TILES + i
            for j in reversed(range(BLOCKS)):

                @pl.when(i >= 0)
                def _():
                    if filtering:
                        if j == 3:
                            fold_stage(flat - 1)
                            pick_stage(0)
                        else:
                            if j == 2:
                                natural_stage(flat - 1)
                            pick_stage(j + 1)
                        filter_stage(i, j)
                        if j == 2:
                            cross_stage(i, 2)
                        if j == 0:
                            cross_stage(i, 0)
                        if j:
                            window_stage(i, j - 1)
                        else:
                            window_stage(jnp.minimum(i + 1, TILES - 1), BLOCKS - 1)
                    if differentiating:
                        element_stage(i, list(reversed(range(j * JOINED, (j + 1) * JOINED))))
                        if j == 1:
                            following = jnp.minimum(i + 1, TILES - 1)
                            input_stage(following)
                            element_stage(following, [GROUPS])
                        if j == 0:
                            totals_stage(i)

            return carry

        return run

    @pl.when(now == 0)
    def _():
        window_stage(0, BLOCKS - 1)
        lax.fori_loop(0, TILES, one_tile(True, False), 0)

    @pl.when(jnp.logical_and(now > 0, now < steps))
    def _():
        window_stage(0, BLOCKS - 1)
        input_stage(0)
        element_stage(0, [GROUPS])
        lax.fori_loop(0, TILES, one_tile(True, True), 0)

    @pl.when(now == steps)
    def _():
        fold_stage(now * TILES - 1)
        pick_stage(0)
        natural_stage(now * TILES - 1)
        input_stage(0)
        element_stage(0, [GROUPS])
        lax.fori_loop(0, TILES, one_tile(False, True), 0)

    @pl.when(step >= 0)
    def _():
        for copy in copies(step, slot):
            copy.start()

    @pl.when(now == steps)
    def _():
        if half == HALVES - 1:
            send_out()
        else:
            sums_out[...] = sums[...]

        @pl.when(steps > 1)
        def _():
            for copy in copies(step - 1, 1 - slot):
                copy.wait()

        for copy in copies(step, slot):
            copy.wait()


def last_kernel(scale, first, second, third, fourth, fs_out, fm_out, short_out, medium_out):
    total = (first[...] + second[...] + third[...] + fourth[...]) * scale
    for out, row in ((fs_out, 8), (fm_out, 17)):
        for n in range(9):
            lanes = slice(n % 3 * LANES, (n % 3 + 1) * LANES)
            out[n // 3 : n // 3 + 1, lanes] = total[row + n : row + n + 1]
    short_out[...] = total[26:33]
    row = lax.broadcasted_iota(jnp.int32, (LANES, LANES), 0)
    lane = lax.broadcasted_iota(jnp.int32, (LANES, LANES), 1)
    flip = jnp.where(row + lane == LANES - 1, 1.0, 0.0).astype(F32)
    medium_out[...] = lax.dot_general(
        total[0:8],
        flip,
        (((1,), (1,)), ((), ())),
        precision=lax.Precision.HIGHEST,
        preferred_element_type=F32,
    )


def columns(rows, first=0):
    width = TILES * LANES
    return pl.BlockSpec((rows, width), lambda j: (0, first + j))


def moved_spec(spec, move):
    return pl.BlockSpec(spec.block_shape, lambda j: spec.index_map(move(j)))


def tiled(rows):
    return pl.BlockSpec((TILES, rows, LANES), lambda j: (j, 0, 0))


def shards(
    residual_in, se_streams, cotangent, feat_short, feat_medium, short_filter, medium_filter_weight
):
    res, streams, g = residual_in[0], se_streams[0], cotangent[0]
    rows, channels = res.shape
    seqs, slabs = lax.axis_size("seq"), lax.axis_size("dp")
    tiles = channels // LANES
    steps = tiles // TILES
    groups = medium_filter_weight.shape[1]
    cut = channels // 2
    strip = lambda x, down: pl.BlockSpec((GROUP, cut), lambda j: (down, 2 * x + j))
    last = rows // GROUP - 1
    before, after = pl.pallas_call(
        rim_kernel,
        grid=(2,),
        in_specs=[strip(x, last) for x in (0, 1, 2, 0)] + [strip(x, 0) for x in (0, 1, 2, 0, 0)],
        out_specs=[pl.BlockSpec((n, cut), lambda j: (0, j)) for n in (EARLIER, LATER)],
        out_shape=[jax.ShapeDtypeStruct((n, channels), BF16) for n in (EARLIER, LATER)],
        scratch_shapes=[pltpu.VMEM((LATER_AT + LATER + 6, LANES), F32)],
        compiler_params=pltpu.CompilerParams(vmem_limit_bytes=VMEM),
        name="rims",
    )(*[streams] * 3, res, *[streams] * 3, res, g)
    before, after = turn(before, "seq", 1), turn(after, "seq", -1)
    seq = lax.axis_index("seq")
    inner = jnp.stack([seq > 0, seq < seqs - 1]).astype(F32)
    bands = pl.BlockSpec((LANES * SPAN, LANES), lambda j: (j, 0))
    lag, ahead = pl.pallas_call(
        toeplitz_kernel,
        grid=(groups // LANES,),
        in_specs=[pl.BlockSpec((LANES, LANES), lambda j: (0, j))],
        out_specs=[bands] * 2,
        out_shape=[jax.ShapeDtypeStruct((groups * SPAN, LANES), BF16)] * 2,
        scratch_shapes=[pltpu.VMEM((LANES, LANES), F32)] * 2,
        name="toeplitz",
    )(medium_filter_weight)
    inner, lag, ahead = lax.optimization_barrier((inner, lag, ahead))
    half_tiles = tiles // HALVES
    half_steps = half_tiles // TILES
    filters = (feat_short,) * 3 + (short_filter,) + (feat_medium,) * 3
    long, ext = rows + 2 * GROUP, rows + GROUP
    saved = [long, ext, ext, long, long]
    in_smem = pl.BlockSpec(memory_space=pltpu.SMEM)
    anywhere = pl.BlockSpec(memory_space=pl.ANY)
    limit = pltpu.CompilerParams(vmem_limit_bytes=VMEM)
    scratch = pltpu.VMEM((FRAME + ext, LANES), F32)
    row_buf = lambda n: pltpu.VMEM((n, LANES), F32)
    behind = lambda spec: moved_spec(spec, lambda j: jnp.maximum(j - 1, 0))
    ahead_of = lambda spec: moved_spec(spec, lambda j: jnp.minimum(j, half_steps - 1))

    def specs_of(half):
        block = lambda n: lambda x: columns(n, x * steps + half * half_steps)
        filter_specs = (
            [block(3)(x) for x in range(3)]
            + [block(short_filter.shape[0])(0)]
            + [block(3)(x) for x in range(3)]
        )
        return block(rows), [block(EARLIER)(0), block(LATER)(0)], filter_specs

    def products(half):
        whole, edge, filter_specs = specs_of(half)
        return pl.pallas_call(
            functools.partial(first_kernel, rows),
            grid=(half_steps,),
            in_specs=[whole(x) for x in range(3)]
            + [whole(0)] * 2
            + edge
            + filter_specs
            + [in_smem],
            out_specs=[tiled(rows), tiled(GROUP), tiled(ext)] + [tiled(n) for n in saved],
            out_shape=[
                jax.ShapeDtypeStruct((half_tiles, n, LANES), BF16)
                for n in [rows, GROUP, ext] + saved
            ],
            scratch_shapes=[scratch] * 7 + [row_buf(LATER_AT + LATER + 6)],
            compiler_params=limit,
            name="products",
        )(*[streams] * 3, res, g, before, after, *filters, inner)

    def gradients(half, made, w_prev, d_next, earlier):
        whole, edge, filter_specs = specs_of(half)
        w_own, w_edge, d_own, *kept = made
        per_step = pl.BlockSpec(
            (TILES * GROUPS * SPAN, LANES), lambda j: (half * half_steps + j, 0)
        )
        raw_sums = jax.ShapeDtypeStruct((half_tiles, 40, LANES), F32)
        all_sums = jax.ShapeDtypeStruct((tiles, 33, LANES), BF16)
        own_sums = pl.BlockSpec((half_tiles, 40, LANES), lambda j: (0, 0, 0))
        own_shares = pl.BlockSpec((tiles, 33, LANES), lambda j: (0, 0, 0))
        last = half == HALVES - 1
        first_in = [whole(x) for x in range(3)] + [whole(0)] + edge
        return pl.pallas_call(
            functools.partial(second_kernel, rows, channels, half),
            grid=(half_steps + 1,),
            in_specs=[behind(spec) for spec in first_in]
            + [
                ahead_of(spec)
                for spec in [tiled(rows), tiled(GROUP), tiled(rows), tiled(ext), tiled(ext)]
                + [per_step] * 2
            ]
            + [behind(spec) for spec in [tiled(n) for n in saved] + filter_specs]
            + [in_smem]
            + ([own_sums, anywhere, anywhere] if half else []),
            out_specs=[behind(whole(0)), anywhere] + [own_shares if last else own_sums],
            out_shape=[
                jax.ShapeDtypeStruct((rows, channels), BF16),
                jax.ShapeDtypeStruct((rows, 3 * channels), BF16),
            ]
            + [all_sums if last else raw_sums],
            input_output_aliases={27: 0, 28: 1} if half else {},
            scratch_shapes=[pltpu.VMEM((2, GROUP + rows, LANES), F32)] * 3
            + [row_buf(GROUP)]
            + [pltpu.VMEM((2, n, LANES), F32) for n in (long, ext)]
            + [row_buf(ext + 8)] * 7
            + [pltpu.VMEM((rows, LANES), BF16)] * 2
            + [pltpu.VMEM((BLOCKS, GROUP, LANES), BF16)] * 2
            + [pltpu.VMEM((2 * TILES, ext, LANES), BF16)] * 2
            + [pltpu.VMEM((GROUPS, 8, LANES), F32)]
            + [pltpu.VMEM((2, LANES + SPAN, BLOCKS * LANES), BF16)] * 2
            + [pltpu.VMEM((2, JOINED * SPAN, 2 * LANES), F32)] * 2
            + [
                pltpu.VMEM((25, 8, LANES), F32),
                pltpu.VMEM((half_tiles, 40, LANES), F32),
                pltpu.VMEM((tiles, 40, LANES), F32),
                pltpu.VMEM((2, 3, rows, TILES * LANES), BF16),
                pltpu.SemaphoreType.DMA((2, 3)),
                row_buf(LATER_AT + LATER + 6),
            ],
            compiler_params=limit,
            name="gradients",
        )(
            *[streams] * 3, g, before, after,
            w_own, w_edge, w_prev, d_own, d_next, lag, ahead,
            *kept, *filters, inner, *earlier
        )

    made, arrived = [], []
    for half in range(HALVES):
        made.append(products(half))
        arrived.append((turn(made[half][0], "seq", 1), turn(made[half][2], "seq", -1)))
    earlier = ()
    for half in range(HALVES):
        grad_res, grad_streams, sums = gradients(half, made[half], *arrived[half], earlier)
        earlier = (sums, grad_res, grad_streams)
    norm_factor = 1.0 / math.sqrt(slabs * seqs * rows)
    parts = lax.all_to_all(sums, "seq", split_axis=0, concat_axis=0, tiled=True)
    share = jnp.sum(parts.astype(F32), axis=0)
    others = [turn(share, "dp", n) for n in range(1, slabs)]
    cols = 3 * channels // tiles
    filter_grads = pl.pallas_call(
        functools.partial(last_kernel, norm_factor),
        out_shape=[
            jax.ShapeDtypeStruct(shape, F32)
            for shape in ((3, cols), (3, cols), (7, LANES), (GROUPS, LANES))
        ],
        compiler_params=limit,
        name="totals",
    )(share, *others)
    return (grad_res[None], grad_streams[None], *filter_grads[:3], filter_grads[3].T)


def solution(mesh):
    placed = (P("dp", "seq", None), P("dp", "seq", None), P("dp", "seq", None), P(), P(), P(), P())
    return jax.shard_map(
        shards,
        mesh=mesh,
        in_specs=placed,
        out_specs=(
            P("dp", "seq", None),
            P("dp", "seq", None),
            P(None, "seq"),
            P(None, "seq"),
            P(None, "seq"),
            P(None, "seq"),
        ),
        check_vma=False,
    )
```

```python
import functools
import math

import jax
import jax.numpy as jnp
from jax import lax
from jax.experimental import pallas as pl
from jax.experimental.pallas import tpu as pltpu
from jax.sharding import PartitionSpec as P

F32 = jnp.float32
BF16 = jnp.bfloat16
LANES = 128
GROUP = 16
GROUPS = LANES // GROUP
SPAN = 32
BLOCKS = LANES // SPAN
JOINED = SPAN // GROUP
EDGE = 10
EARLIER_ROWS = ((20, 4), (0, 10), (10, 10), (24, 2))
EARLIER = 26
LATER = 5 * EDGE
LATER_AT = 32
FRAME = 24
HALVES = 1
VMEM = 65408 * 1024
TILES = 4


def turn(array, axis, by):
    peers = lax.axis_size(axis)
    return lax.ppermute(array, axis, [(i, (i + by) % peers) for i in range(peers)])


def lane_blocks(shape):
    return lax.broadcasted_iota(jnp.int32, shape, 1) // SPAN


def swap_blocks(parts):
    parts = list(parts)
    block = lane_blocks(parts[0].shape)
    step = BLOCKS // 2
    while step:
        low = (block & step) == 0
        shift = SPAN * step
        for i in range(BLOCKS):
            if i & step == 0:
                first, second = parts[i], parts[i + step]
                parts[i] = jnp.where(low, first, pltpu.roll(second, shift, 1))
                parts[i + step] = jnp.where(low, pltpu.roll(first, LANES - shift, 1), second)
        step //= 2
    return parts


def taps_of(ref, lanes):
    return [ref[i : i + 1, lanes] for i in range(ref.shape[0])]


def back_taps(taps, ref, start, rows):
    total = taps[0] * ref[start : start + rows, :]
    for i in range(1, len(taps)):
        total = total + taps[i] * ref[start - i : start - i + rows, :]
    return total


def ahead_taps(taps, ref, start, rows):
    total = taps[0] * ref[start : start + rows, :]
    for i in range(1, len(taps)):
        total = total + taps[i] * ref[start + i : start + i + rows, :]
    return total


def rim_kernel(lq, lk, lv, lr, fq, fk, fv, fr, fg, before, after, rim):
    for c in range(0, before.shape[1], LANES):
        lanes = slice(c, c + LANES)
        for at, ref in ((16, lr), (14, lq), (10, lv), (0, lk)):
            rim[at : at + GROUP, :] = ref[:, lanes].astype(F32)
        before[:, lanes] = rim[GROUP - EDGE : GROUP - EDGE + EARLIER, :].astype(BF16)
        for x, ref in enumerate((fq, fk, fv, fr, fg)):
            at = LATER_AT + EDGE * x
            rim[at : at + GROUP, :] = ref[:, lanes].astype(F32)
        after[:, lanes] = rim[LATER_AT : LATER_AT + LATER, :].astype(BF16)


def first_kernel(rows, *refs):
    (q, k, v, res, g, before, after) = refs[:7]
    (fsq, fsk, fsv, short, fmq, fmk, fmv, inner) = refs[7:15]
    (w_own, w_edge, d_own, mid_out, q1_out, s1_out, k1_out, v1_out) = refs[15:23]
    (sq, sk, sv, sr, sg, sw, sm, rim) = refs[23:]
    total = rows + GROUP

    @pl.when(pl.program_id(0) == 0)
    def _():
        for ref in (sq, sk, sv, sr, sg):
            ref[...] = jnp.zeros(ref.shape, F32)

    def one_tile(i, carry):
        lanes = pl.ds(pl.multiple_of(i * LANES, LANES), LANES)
        rim[0:EARLIER, :] = before[:, lanes].astype(F32) * inner[0]
        rim[LATER_AT : LATER_AT + LATER, :] = after[:, lanes].astype(F32) * inner[1]
        for x, (scratch, own) in enumerate(((sq, q), (sk, k), (sv, v), (sr, res), (sg, g))):
            if x < 4:
                at, count = EARLIER_ROWS[x]
                scratch[FRAME - count : FRAME, :] = rim[at : at + count, :]
            for r in range(0, rows, GROUP):
                scratch[FRAME + r : FRAME + r + GROUP, :] = own[r : r + GROUP, lanes].astype(F32)
            at = LATER_AT + EDGE * x
            scratch[FRAME + rows : FRAME + rows + EDGE, :] = rim[at : at + EDGE, :]
        tq, tk, tv = taps_of(fsq, lanes), taps_of(fsk, lanes), taps_of(fsv, lanes)
        for t in range(-GROUP, total, GROUP):
            at = FRAME + t
            k1 = back_taps(tk, sk, at, GROUP)
            v1 = back_taps(tv, sv, at, GROUP)
            sw[at : at + GROUP, :] = k1 * v1
            k1_out[i, t + GROUP : t + 2 * GROUP, :] = k1.astype(BF16)
            v1_out[i, t + GROUP : t + 2 * GROUP, :] = v1.astype(BF16)
        ts = taps_of(short, lanes)
        for t in range(-GROUP, total, GROUP):
            at = FRAME + t
            q1 = back_taps(tq, sq, at, GROUP)
            s1 = back_taps(ts, sw, at, GROUP)
            mid = (sr[at : at + GROUP, :] + q1 * s1).astype(BF16)
            sm[at : at + GROUP, :] = mid.astype(F32)
            mid_out[i, t + GROUP : t + 2 * GROUP, :] = mid
            if t >= 0:
                q1_out[i, t : t + GROUP, :] = q1.astype(BF16)
                s1_out[i, t : t + GROUP, :] = s1.astype(BF16)
        mq, mk, mv = taps_of(fmq, lanes), taps_of(fmk, lanes), taps_of(fmv, lanes)
        products, slopes = [], []
        for t in range(0, total, GROUP):
            at = FRAME + t
            m = [sm[at - j : at - j + GROUP, :] for j in range(3)]
            q2, k2, v2 = [
                taps[0] * m[0] + taps[1] * m[1] + taps[2] * m[2] for taps in (mq, mk, mv)
            ]
            products.append((k2 * v2).astype(BF16))
            slopes.append((sg[at : at + GROUP, :] * q2).astype(BF16))
        for values, own in ((products, w_own), (slopes, d_own)):
            parts = [
                jnp.concatenate(values[j : j + JOINED], 0)
                for j in range(0, GROUPS, JOINED)
            ]
            for j, part in enumerate(swap_blocks(parts)):
                own[i, j * SPAN : (j + 1) * SPAN, :] = part
        w_edge[i] = products[GROUPS]
        d_own[i, rows : rows + GROUP, :] = slopes[GROUPS]
        return carry

    lax.fori_loop(0, TILES, one_tile, 0, unroll=True)


def windows(low, high, last, block):
    rows = []
    for k in range(BLOCKS + 1):
        if k == 0:
            first, second = low, high
        elif k == BLOCKS:
            first, second = high, last
        else:
            shift = LANES - SPAN * k
            second = pltpu.roll(high, shift, 1)
            first = jnp.where(block < BLOCKS - k, pltpu.roll(low, shift, 1), second)
        rows.append(jnp.concatenate([first, second], 1))
    return jnp.concatenate(rows, 0)


def fold_diagonals(parts):
    row = lax.broadcasted_iota(jnp.int32, parts[0].shape, 0)
    half = len(parts) // 2
    while half:
        first = (row & half) == 0
        folded = []
        for x, y in zip(parts[:half], parts[half:]):
            low = jnp.where(first, x, pltpu.roll(y, half, 0))
            high = jnp.where(first, pltpu.roll(x, 8 - half, 0), y)
            folded.append(low + pltpu.roll(high, LANES - half, 1))
        parts = folded
        half //= 2
    return parts[0]


def fold_rows(parts):
    row = lax.broadcasted_iota(jnp.int32, parts[0].shape, 0)
    half = len(parts) // 2
    while half:
        first = (row & half) == 0
        parts = [
            jnp.where(first, x, pltpu.roll(y, half, 0))
            + jnp.where(first, pltpu.roll(x, 8 - half, 0), y)
            for x, y in zip(parts[:half], parts[half:])
        ]
        half //= 2
    return parts[0]


def toeplitz_kernel(taps, lag_out, ahead_out, taps_fwd, taps_rev):
    row = lax.broadcasted_iota(jnp.int32, (LANES, LANES), 0)
    lane = lax.broadcasted_iota(jnp.int32, (LANES, LANES), 1)
    for out, places in ((taps_fwd, row == lane), (taps_rev, row + lane == LANES - 1)):
        out[...] = lax.dot_general(
            taps[...],
            jnp.where(places, 1.0, 0.0).astype(BF16),
            (((0,), (0,)), ((), ())),
            preferred_element_type=F32,
        )
    shape = (SPAN, LANES)
    for j in range(LANES):
        part = slice(j * SPAN, (j + 1) * SPAN)
        for taps, first, out in ((taps_fwd, 0, ahead_out), (taps_rev, 1, lag_out)):
            turned = pltpu.roll(
                jnp.broadcast_to(taps[j : j + 1, :], shape), first, 1, stride=1, stride_axis=0
            )
            out[part, :] = turned.astype(BF16)


def second_kernel(rows, channels, half, *refs):
    (q, k, v, g, before, after) = refs[:6]
    rim, refs = refs[-1], (None, None) + refs[:-1]
    (w_own, w_edge, w_prev, d_own, d_next, lag_in, ahead_in) = refs[8:15]
    (mid_in, q1_in, s1_in, k1_in, v1_in) = refs[15:20]
    (fsq, fsk, fsv, short, fmq, fmk, fmv, inner) = refs[20:28]
    if half:
        earlier, refs = refs[28], refs[:28] + refs[31:]
    (grad_res, grad_streams, sums_out) = refs[28:31]
    refs = refs[:27] + refs[28:]
    (sq, sk, sv, sg, sm, sw, dq, dk, dv, d1, eq, ek, ev) = refs[30:43]
    (s2_apart, w2_apart, s2_ends, w2_ends, s2_nat, w2_nat, diagonals, wins, d_wins) = refs[43:52]
    (s2_raw, w2_raw, acc, sums, moved, out_buf, sems) = refs[52:]
    now = pl.program_id(0)
    steps = pl.num_programs(0) - 1
    step = now - 1
    slot = lax.rem(now + 1, 2)
    width = TILES * LANES
    base = GROUP
    block = lane_blocks((SPAN, LANES))
    zero = jnp.zeros((), BF16)

    def copies(at_step, at_slot):
        return [
            pltpu.make_async_copy(
                out_buf.at[at_slot, x],
                grad_streams.at[
                    :,
                    pl.ds(
                        pl.multiple_of(x * channels + (half * steps + at_step) * width, width),
                        width,
                    ),
                ],
                sems.at[at_slot, x],
            )
            for x in range(3)
        ]

    def lanes_of(i):
        return pl.ds(pl.multiple_of(i * LANES, LANES), LANES)

    def slot_of(n):
        return lax.broadcasted_iota(jnp.int32, (n, LANES), 1) // GROUP % JOINED

    def pick(wide, count, lanes):
        out = wide[:count, lanes]
        for n in range(1, JOINED):
            out = jnp.where(slot_of(count) == n, wide[n * SPAN : n * SPAN + count, lanes], out)
        return out

    def window_stage(i, j):
        part = slice(j * SPAN, (j + 1) * SPAN)
        no_rows = jnp.zeros((SPAN - GROUP, LANES), BF16)
        keep = [jnp.full((SPAN, LANES), inner[n], F32).astype(BF16) for n in range(2)]
        last_w = w_edge[i]
        last_d = d_next[i, rows : rows + GROUP, :] * keep[1][:GROUP]
        if j:
            last_w = pltpu.roll(last_w, LANES - SPAN * j, 1)
            last_d = pltpu.roll(last_d, LANES - SPAN * j, 1)
        for low, high, last, out in (
            (w_prev[i, part, :] * keep[0], w_own[i, part, :], last_w, wins),
            (d_own[i, part, :], d_next[i, part, :] * keep[1], last_d, d_wins),
        ):
            win = windows(low, high, jnp.concatenate([last, no_rows], 0), block)
            for n in range(2):
                out[n, :, j * LANES : (j + 1) * LANES] = win[:, n * LANES : (n + 1) * LANES]

    def filter_stage(i, j):
        taps_part = pl.ds((i * BLOCKS + j) * JOINED * SPAN, JOINED * SPAN)
        row = lax.broadcasted_iota(jnp.int32, (JOINED * SPAN, LANES), 0) % SPAN
        lane = lax.broadcasted_iota(jnp.int32, (JOINED * SPAN, LANES), 1)
        for bands, inside, win, raw in (
            (lag_in, lane > row, wins, s2_raw),
            (ahead_in, lane >= row, d_wins, w2_raw),
        ):
            at = slice(j * LANES, (j + 1) * LANES)
            turned = bands[taps_part, :]
            over = jnp.where(inside, zero, turned)[:, :SPAN]
            raw[j % 2] = jnp.dot(
                jnp.concatenate([jnp.where(inside, turned, zero), over], 1),
                jnp.concatenate([win[0, :, at], win[1, :, at]], 1),
                preferred_element_type=F32,
            )

    def pick_stage(j):
        part = slice(j * SPAN, (j + 1) * SPAN)
        main, edge = slice(0, LANES), slice(LANES, 2 * LANES)
        for raw, apart_ref, ends_ref in ((s2_raw, s2_apart, s2_ends), (w2_raw, w2_apart, w2_ends)):
            value = raw[j % 2].astype(BF16)
            apart_ref[part, :] = pick(value, SPAN, main)
            end = pick(value, GROUP, edge)
            ends_ref[j] = pltpu.roll(end, SPAN * j, 1) if j else end

    def cross_stage(i, first):
        row = lax.broadcasted_iota(jnp.int32, (SPAN, LANES), 0)
        lane = lax.broadcasted_iota(jnp.int32, (SPAN, LANES), 1)
        nothing = jnp.zeros((SPAN, LANES), BF16)
        apart = []
        for j in (first, first + 1):
            own_d = d_own[i, j * SPAN : (j + 1) * SPAN, :]
            for n in range(JOINED):
                mine = jnp.where(slot_of(SPAN) == n, own_d, zero)
                pair = [mine, nothing] if j == first else [nothing, mine]
                apart.append(jnp.concatenate(pair, 1))
        cross = lax.dot_general(
            jnp.concatenate(apart, 0),
            wins[0, :, first * LANES : (first + 2) * LANES],
            (((1,), (1,)), ((), ())),
            preferred_element_type=F32,
        )
        for n in range(2 * JOINED):
            mine = cross[n * SPAN : (n + 1) * SPAN]
            over = jnp.concatenate(
                [mine[:, LANES:], jnp.zeros((SPAN, LANES - SPAN), F32)], 1
            )
            mine = jnp.where(lane <= row, over, mine[:, :LANES])
            diagonals[first * JOINED + n] = sum(
                pltpu.roll(mine[r : r + 8], LANES - 1 - r, 1) for r in range(0, SPAN, 8)
            )

    def natural_stage(f):
        place = lax.rem(f + 2 * TILES, 2 * TILES)
        for apart_ref, ends_ref, nat in ((s2_apart, s2_ends, s2_nat), (w2_apart, w2_ends, w2_nat)):
            parts = swap_blocks([apart_ref[j * SPAN : (j + 1) * SPAN, :] for j in range(BLOCKS)])
            for j in range(BLOCKS):
                nat[place, j * SPAN : (j + 1) * SPAN, :] = parts[j]
            end = ends_ref[0]
            for j in range(1, BLOCKS):
                end = jnp.where(lane_blocks((GROUP, LANES)) == j, ends_ref[j], end)
            nat[place, rows : rows + GROUP, :] = end

    def fold_stage(f):
        sums[pl.ds(jnp.maximum(f, 0), 1), :GROUPS, :] = fold_diagonals(
            [diagonals[j] for j in range(GROUPS)]
        )[None]

    def input_stage(i):
        lanes = lanes_of(i)
        par = lax.rem(i, 2)
        for r in range(0, rows + 2 * GROUP, GROUP):
            sm[par, r : r + GROUP, :] = mid_in[i, r : r + GROUP, :].astype(F32)
        for r in range(0, rows + GROUP, GROUP):
            sw[par, r : r + GROUP, :] = k1_in[i, r : r + GROUP, :].astype(F32) * v1_in[
                i, r : r + GROUP, :
            ].astype(F32)
        rim[0:EARLIER, :] = before[:, lanes].astype(F32) * inner[0]
        rim[LATER_AT : LATER_AT + LATER, :] = after[:, lanes].astype(F32) * inner[1]
        for x, (scratch, own) in enumerate(((sq, q), (sk, k), (sv, v))):
            at, count = EARLIER_ROWS[x]
            scratch[par, base - 2 : base, :] = rim[at + count - 2 : at + count, :]
            for r in range(0, rows, GROUP):
                scratch[par, base + r : base + r + GROUP, :] = own[r : r + GROUP, lanes].astype(F32)
        sg[0:EDGE, :] = rim[LATER_AT + 4 * EDGE : LATER_AT + LATER, :]

    def add_up(first, values, others, fresh):
        for n, other in enumerate(others):
            total = None
            for x, y in zip(values, other):
                product = x * y
                for r in range(0, GROUP, 8):
                    half = product[r : r + 8]
                    total = half if total is None else total + half
            acc[first + n] = total if fresh else acc[first + n] + total

    def element_stage(i, chunks):
        lanes = lanes_of(i)
        par = lax.rem(i, 2)
        place = lax.rem(step * TILES + i + 2 * TILES, 2 * TILES)
        main = chunks[0] < GROUPS
        fresh = chunks[0] == GROUPS - 1
        mq, mk, mv = taps_of(fmq, lanes), taps_of(fmk, lanes), taps_of(fmv, lanes)
        starts = [a * GROUP for a in chunks]
        at = lambda ref, t: ref[t : t + GROUP, :]
        gs = [g[t : t + GROUP, lanes].astype(F32) if main else sg[...] for t in starts]
        tall = lambda ref, t: ref[par, t : t + GROUP, :]
        mids = [[tall(sm, base + t - n) for t in starts] for n in range(3)]
        parts = [[], [], []]
        for c, t in enumerate(starts):
            m = [mids[n][c] for n in range(3)]
            k2 = mk[0] * m[0] + mk[1] * m[1] + mk[2] * m[2]
            v2 = mv[0] * m[0] + mv[1] * m[1] + mv[2] * m[2]
            s2 = s2_nat[place, t : t + GROUP, :].astype(F32)
            w2 = w2_nat[place, t : t + GROUP, :].astype(F32)
            for x, (ref, value) in enumerate(
                zip((dq, dk, dv), (gs[c] * s2, w2 * v2, w2 * k2))
            ):
                ref[t : t + GROUP, :] = value
                parts[x].append(value)
        if main:
            for x in range(3):
                add_up(9 + 3 * x, parts[x], mids, fresh)
        slopes = []
        for c, t in enumerate(starts):
            dmid = (
                gs[c]
                + ahead_taps(mq, dq, t, GROUP)
                + ahead_taps(mk, dk, t, GROUP)
                + ahead_taps(mv, dv, t, GROUP)
            )
            if main:
                grad_res[t : t + GROUP, lanes] = dmid.astype(BF16)
            slope = dmid * q1_in[i, t : t + GROUP, :].astype(F32)
            d1[t : t + GROUP, :] = slope
            slopes.append(slope)
            eq[t : t + GROUP, :] = dmid * s1_in[i, t : t + GROUP, :].astype(F32)
        ts = taps_of(short, lanes)
        if main:
            lagged = [[tall(sw, base + t - n) for t in starts] for n in range(len(ts))]
            add_up(18, slopes, lagged, fresh)
        for t in starts:
            dw1 = ahead_taps(ts, d1, t, GROUP)
            ek[t : t + GROUP, :] = dw1 * v1_in[i, base + t : base + t + GROUP, :].astype(F32)
            ev[t : t + GROUP, :] = dw1 * k1_in[i, base + t : base + t + GROUP, :].astype(F32)
        if not main:
            return
        for x, (ref, taps_ref, stream) in enumerate(((eq, fsq, sq), (ek, fsk, sk), (ev, fsv, sv))):
            taps = taps_of(taps_ref, lanes)
            for t in starts:
                out_buf[slot, x, t : t + GROUP, lanes] = ahead_taps(taps, ref, t, GROUP).astype(
                    BF16
                )
            add_up(
                3 * x,
                [at(ref, t) for t in starts],
                [[tall(stream, base + t - n) for t in starts] for n in range(3)],
                fresh,
            )

    def totals_stage(i):
        tile = pl.ds(jnp.maximum(step * TILES + i, 0), 1)
        for n in range(0, 24, 8):
            sums[tile, GROUPS + n : GROUPS + n + 8, :] = fold_rows(
                [acc[n + j] for j in range(8)]
            )[None]
        sums[tile, 32:33, :] = jnp.sum(acc[24], axis=0, keepdims=True)[None]

    @pl.when(now == 0)
    def _():
        for ref in (sg, dq, dk, dv, d1, eq, ek, ev):
            ref[...] = jnp.zeros(ref.shape, F32)

    @pl.when(step >= 2)
    def _():
        for copy in copies(step - 2, slot):
            copy.wait()

    def send_out():
        tiles = sums.shape[0]
        of = lambda tile: earlier if half and tile < tiles else sums
        for to in range(moved.shape[0]):
            for place in range(3):
                x, tile = divmod(3 * to + place, moved.shape[0])
                for n in range(3):
                    for row in (GROUPS, GROUPS + 9):
                        at, source = row + 3 * n + place, row + 3 * x + n
                        moved[to, at : at + 1, :] = of(tile)[
                            tile % tiles, source : source + 1, :
                        ]
            moved[to, :GROUPS, :] = of(to)[to % tiles, :GROUPS, :]
            moved[to, 26:33, :] = of(to)[to % tiles, 26:33, :]
        sums_out[...] = moved[:, :33, :].astype(BF16)

    def one_tile(filtering, differentiating):
        def run(i, carry):
            flat = now * TILES + i
            for j in reversed(range(BLOCKS)):

                @pl.when(i >= 0)
                def _():
                    if filtering:
                        if j == 3:
                            fold_stage(flat - 1)
                            pick_stage(0)
                        else:
                            if j == 2:
                                natural_stage(flat - 1)
                            pick_stage(j + 1)
                        filter_stage(i, j)
                        if j == 2:
                            cross_stage(i, 2)
                        if j == 0:
                            cross_stage(i, 0)
                        if j:
                            window_stage(i, j - 1)
                        else:
                            window_stage(jnp.minimum(i + 1, TILES - 1), BLOCKS - 1)
                    if differentiating:
                        element_stage(i, list(reversed(range(j * JOINED, (j + 1) * JOINED))))
                        if j == 1:
                            following = jnp.minimum(i + 1, TILES - 1)
                            input_stage(following)
                            element_stage(following, [GROUPS])
                        if j == 0:
                            totals_stage(i)

            return carry

        return run

    @pl.when(now == 0)
    def _():
        window_stage(0, BLOCKS - 1)
        lax.fori_loop(0, TILES, one_tile(True, False), 0)

    @pl.when(jnp.logical_and(now > 0, now < steps))
    def _():
        window_stage(0, BLOCKS - 1)
        input_stage(0)
        element_stage(0, [GROUPS])
        lax.fori_loop(0, TILES, one_tile(True, True), 0)

    @pl.when(now == steps)
    def _():
        fold_stage(now * TILES - 1)
        pick_stage(0)
        natural_stage(now * TILES - 1)
        input_stage(0)
        element_stage(0, [GROUPS])
        lax.fori_loop(0, TILES, one_tile(False, True), 0)

    @pl.when(step >= 0)
    def _():
        for copy in copies(step, slot):
            copy.start()

    @pl.when(now == steps)
    def _():
        if half == HALVES - 1:
            send_out()
        else:
            sums_out[...] = sums[...]

        @pl.when(steps > 1)
        def _():
            for copy in copies(step - 1, 1 - slot):
                copy.wait()

        for copy in copies(step, slot):
            copy.wait()


def last_kernel(scale, first, second, third, fourth, fs_out, fm_out, short_out, medium_out):
    total = (first[...] + second[...] + third[...] + fourth[...]) * scale
    for out, row in ((fs_out, 8), (fm_out, 17)):
        for n in range(9):
            lanes = slice(n % 3 * LANES, (n % 3 + 1) * LANES)
            out[n // 3 : n // 3 + 1, lanes] = total[row + n : row + n + 1]
    short_out[...] = total[26:33]
    row = lax.broadcasted_iota(jnp.int32, (LANES, LANES), 0)
    lane = lax.broadcasted_iota(jnp.int32, (LANES, LANES), 1)
    flip = jnp.where(row + lane == LANES - 1, 1.0, 0.0).astype(F32)
    medium_out[...] = lax.dot_general(
        total[0:8],
        flip,
        (((1,), (1,)), ((), ())),
        precision=lax.Precision.HIGHEST,
        preferred_element_type=F32,
    )


def columns(rows, first=0):
    width = TILES * LANES
    return pl.BlockSpec((rows, width), lambda j: (0, first + j))


def moved_spec(spec, move):
    return pl.BlockSpec(spec.block_shape, lambda j: spec.index_map(move(j)))


def tiled(rows):
    return pl.BlockSpec((TILES, rows, LANES), lambda j: (j, 0, 0))


def shards(
    residual_in, se_streams, cotangent, feat_short, feat_medium, short_filter, medium_filter_weight
):
    res, streams, g = residual_in[0], se_streams[0], cotangent[0]
    rows, channels = res.shape
    seqs, slabs = lax.axis_size("seq"), lax.axis_size("dp")
    tiles = channels // LANES
    steps = tiles // TILES
    groups = medium_filter_weight.shape[1]
    cut = channels // 2
    strip = lambda x, down: pl.BlockSpec((GROUP, cut), lambda j: (down, 2 * x + j))
    last = rows // GROUP - 1
    before, after = pl.pallas_call(
        rim_kernel,
        grid=(2,),
        in_specs=[strip(x, last) for x in (0, 1, 2, 0)] + [strip(x, 0) for x in (0, 1, 2, 0, 0)],
        out_specs=[pl.BlockSpec((n, cut), lambda j: (0, j)) for n in (EARLIER, LATER)],
        out_shape=[jax.ShapeDtypeStruct((n, channels), BF16) for n in (EARLIER, LATER)],
        scratch_shapes=[pltpu.VMEM((LATER_AT + LATER + 6, LANES), F32)],
        compiler_params=pltpu.CompilerParams(vmem_limit_bytes=VMEM),
        name="rims",
    )(*[streams] * 3, res, *[streams] * 3, res, g)
    before, after = turn(before, "seq", 1), turn(after, "seq", -1)
    seq = lax.axis_index("seq")
    inner = jnp.stack([seq > 0, seq < seqs - 1]).astype(F32)
    bands = pl.BlockSpec((LANES * SPAN, LANES), lambda j: (j, 0))
    lag, ahead = pl.pallas_call(
        toeplitz_kernel,
        grid=(groups // LANES,),
        in_specs=[pl.BlockSpec((LANES, LANES), lambda j: (0, j))],
        out_specs=[bands] * 2,
        out_shape=[jax.ShapeDtypeStruct((groups * SPAN, LANES), BF16)] * 2,
        scratch_shapes=[pltpu.VMEM((LANES, LANES), F32)] * 2,
        name="toeplitz",
    )(medium_filter_weight)
    inner, lag, ahead = lax.optimization_barrier((inner, lag, ahead))
    half_tiles = tiles // HALVES
    half_steps = half_tiles // TILES
    filters = (feat_short,) * 3 + (short_filter,) + (feat_medium,) * 3
    long, ext = rows + 2 * GROUP, rows + GROUP
    saved = [long, ext, ext, long, long]
    in_smem = pl.BlockSpec(memory_space=pltpu.SMEM)
    anywhere = pl.BlockSpec(memory_space=pl.ANY)
    limit = pltpu.CompilerParams(vmem_limit_bytes=VMEM)
    scratch = pltpu.VMEM((FRAME + ext, LANES), F32)
    row_buf = lambda n: pltpu.VMEM((n, LANES), F32)
    behind = lambda spec: moved_spec(spec, lambda j: jnp.maximum(j - 1, 0))
    ahead_of = lambda spec: moved_spec(spec, lambda j: jnp.minimum(j, half_steps - 1))

    def specs_of(half):
        block = lambda n: lambda x: columns(n, x * steps + half * half_steps)
        filter_specs = (
            [block(3)(x) for x in range(3)]
            + [block(short_filter.shape[0])(0)]
            + [block(3)(x) for x in range(3)]
        )
        return block(rows), [block(EARLIER)(0), block(LATER)(0)], filter_specs

    def products(half):
        whole, edge, filter_specs = specs_of(half)
        return pl.pallas_call(
            functools.partial(first_kernel, rows),
            grid=(half_steps,),
            in_specs=[whole(x) for x in range(3)]
            + [whole(0)] * 2
            + edge
            + filter_specs
            + [in_smem],
            out_specs=[tiled(rows), tiled(GROUP), tiled(ext)] + [tiled(n) for n in saved],
            out_shape=[
                jax.ShapeDtypeStruct((half_tiles, n, LANES), BF16)
                for n in [rows, GROUP, ext] + saved
            ],
            scratch_shapes=[scratch] * 7 + [row_buf(LATER_AT + LATER + 6)],
            compiler_params=limit,
            name="products",
        )(*[streams] * 3, res, g, before, after, *filters, inner)

    def gradients(half, made, w_prev, d_next, earlier):
        whole, edge, filter_specs = specs_of(half)
        w_own, w_edge, d_own, *kept = made
        per_step = pl.BlockSpec(
            (TILES * GROUPS * SPAN, LANES), lambda j: (half * half_steps + j, 0)
        )
        raw_sums = jax.ShapeDtypeStruct((half_tiles, 40, LANES), F32)
        all_sums = jax.ShapeDtypeStruct((tiles, 33, LANES), BF16)
        own_sums = pl.BlockSpec((half_tiles, 40, LANES), lambda j: (0, 0, 0))
        own_shares = pl.BlockSpec((tiles, 33, LANES), lambda j: (0, 0, 0))
        last = half == HALVES - 1
        first_in = [whole(x) for x in range(3)] + [whole(0)] + edge
        return pl.pallas_call(
            functools.partial(second_kernel, rows, channels, half),
            grid=(half_steps + 1,),
            in_specs=[behind(spec) for spec in first_in]
            + [
                ahead_of(spec)
                for spec in [tiled(rows), tiled(GROUP), tiled(rows), tiled(ext), tiled(ext)]
                + [per_step] * 2
            ]
            + [behind(spec) for spec in [tiled(n) for n in saved] + filter_specs]
            + [in_smem]
            + ([own_sums, anywhere, anywhere] if half else []),
            out_specs=[behind(whole(0)), anywhere] + [own_shares if last else own_sums],
            out_shape=[
                jax.ShapeDtypeStruct((rows, channels), BF16),
                jax.ShapeDtypeStruct((rows, 3 * channels), BF16),
            ]
            + [all_sums if last else raw_sums],
            input_output_aliases={27: 0, 28: 1} if half else {},
            scratch_shapes=[pltpu.VMEM((2, GROUP + rows, LANES), F32)] * 3
            + [row_buf(GROUP)]
            + [pltpu.VMEM((2, n, LANES), F32) for n in (long, ext)]
            + [row_buf(ext + 8)] * 7
            + [pltpu.VMEM((rows, LANES), BF16)] * 2
            + [pltpu.VMEM((BLOCKS, GROUP, LANES), BF16)] * 2
            + [pltpu.VMEM((2 * TILES, ext, LANES), BF16)] * 2
            + [pltpu.VMEM((GROUPS, 8, LANES), F32)]
            + [pltpu.VMEM((2, LANES + SPAN, BLOCKS * LANES), BF16)] * 2
            + [pltpu.VMEM((2, JOINED * SPAN, 2 * LANES), F32)] * 2
            + [
                pltpu.VMEM((25, 8, LANES), F32),
                pltpu.VMEM((half_tiles, 40, LANES), F32),
                pltpu.VMEM((tiles, 40, LANES), F32),
                pltpu.VMEM((2, 3, rows, TILES * LANES), BF16),
                pltpu.SemaphoreType.DMA((2, 3)),
                row_buf(LATER_AT + LATER + 6),
            ],
            compiler_params=limit,
            name="gradients",
        )(
            *[streams] * 3, g, before, after,
            w_own, w_edge, w_prev, d_own, d_next, lag, ahead,
            *kept, *filters, inner, *earlier
        )

    made, arrived = [], []
    for half in range(HALVES):
        made.append(products(half))
        arrived.append((turn(made[half][0], "seq", 1), turn(made[half][2], "seq", -1)))
    earlier = ()
    for half in range(HALVES):
        grad_res, grad_streams, sums = gradients(half, made[half], *arrived[half], earlier)
        earlier = (sums, grad_res, grad_streams)
    norm_factor = 1.0 / math.sqrt(slabs * seqs * rows)
    parts = lax.all_to_all(sums, "seq", split_axis=0, concat_axis=0, tiled=True)
    share = jnp.sum(parts.astype(F32), axis=0)
    others = [turn(share, "dp", n) for n in range(1, slabs)]
    cols = 3 * channels // tiles
    filter_grads = pl.pallas_call(
        functools.partial(last_kernel, norm_factor),
        out_shape=[
            jax.ShapeDtypeStruct(shape, F32)
            for shape in ((3, cols), (3, cols), (7, LANES), (GROUPS, LANES))
        ],
        compiler_params=limit,
        name="totals",
    )(share, *others)
    return (grad_res[None], grad_streams[None], *filter_grads[:3], filter_grads[3].T)


def solution(mesh):
    placed = (P("dp", "seq", None), P("dp", "seq", None), P("dp", "seq", None), P(), P(), P(), P())
    return jax.shard_map(
        shards,
        mesh=mesh,
        in_specs=placed,
        out_specs=(
            P("dp", "seq", None),
            P("dp", "seq", None),
            P(None, "seq"),
            P(None, "seq"),
            P(None, "seq"),
            P(None, "seq"),
        ),
        check_vma=False,
    )
```
